256 devices in a mesh: spec: 16 (over z, x_lo), line: 4 (over y), lay: 4 (over x_hi, core).
Axes of the slice: x: 4 (x_hi: 2, x_lo: 2; x = x_hi * 2 + x_lo), y: 4, z: 8, core: 2. Of those that a mesh axis runs over, the one named last changes fastest.
Arguments:
- line_offset: float32 [262144], P(('spec', 'line')), may hold values from 0 to 256
- line_strength: float32 [262144], P(('spec', 'line')), may hold values from 0.2 to 5
- lower_energy: float32 [262144], P(('spec', 'line')), may hold values from 20 to 2000
- lorentz_width: float32 [262144], P(('spec', 'line')), may hold values from 4 to 60
- doppler_width: float32 [262144], P(('spec', 'line')), may hold values from 2 to 12
- line_species: int32 [262144], P(('spec', 'line')), may hold values from 0 to 2
- cutoff: int32 [2048, 4], P(('spec', 'line')), may hold values from -1 to 255, as said below
- layer_pressure: float32 [8], P('lay'), may hold values from 0.1 to 1
- layer_temp: float32 [8], P('lay'), may hold values from 200 to 300
- column_index: int32 [32, 8], replicated, may hold values from 0 to 63
- column_table: float32 [3, 64], replicated, may hold values from 0.03 to 0.3
- noise_var: float32 [65536], P(('spec', 'line')), may hold values from 1e-05 to 0.0004
Outputs:
- transmit: float32 [32, 65536], P(None, ('spec', 'line'))
- normals: float32 [32, 24, 24], P(None, 'lay')
The draws below stay inside these ranges and needn't reach their ends.
Inputs may be any that keep to these rules, and one draw needn't show every extreme that they name: `cutoff`: blocks are numbered in order, 32 to each index d of spec+line; tile t belongs to index t // 4. A block's entries that are not -1 come first, are distinct, and name tiles of indices d - 1, d and d + 1; every block has at least one such entry, some have 4.
All inputs are finite; a program needn't handle non-finite values.
Results may differ from the reference program's by a relative error of at most 0.0003.
Values sent between devices are 32-bit elements; how exact they have to be, the bound alone decides.
No kernel may reach another device: no remote copies, remote signals or barrier semaphores. Data moves between devices by JAX's collectives and lax.ppermute only.
A program may use at most 192 MiB of HBM per device.

```python
import math
import jax
import jax.numpy as jnp
from jax import lax

TILE = 256
NEAR = 4
LBLK = 128
BLK_DEV = 32
TILES_DEV = 4
SPECIES = 3
SOUND = 32
NCOL = 64
LAYERS = 8
BLOCKS = 2048
LINES = 262144
NT = 256
NU = 65536
N_SPEC = 16
N_LINE = 4


def draw_cutoff(key, part):
    key = jax.random.fold_in(key, 11)
    score_key, count_key = jax.random.split(key)
    groups = N_SPEC * N_LINE
    owner = jnp.arange(BLOCKS, dtype=jnp.int32) // BLK_DEV
    block_slot = jnp.arange(BLOCKS, dtype=jnp.int32) % BLK_DEV
    low_tile = jnp.maximum(owner - 1, 0) * TILES_DEV
    high_tile = jnp.minimum(owner + 2, groups) * TILES_DEV
    tile_span = high_tile - low_tile
    candidate = jnp.arange(3 * TILES_DEV, dtype=jnp.int32)
    scores = jax.random.randint(score_key, (BLOCKS, 3 * TILES_DEV), 0, 1 << 18, dtype=jnp.int32) * 4096 + candidate[None, :]
    scores = jnp.where(candidate[None, :] < tile_span[:, None], scores, -1 - candidate[None, :])
    scores = jnp.where((block_slot[:, None] == 0) & (candidate[None, :] == tile_span[:, None] - 1), (1 << 30) + 1, scores)
    picked = lax.top_k(scores, NEAR)[1].astype(jnp.int32)
    tiles_named = low_tile[:, None] + picked
    valid_count = jax.random.randint(count_key, (BLOCKS,), 1, NEAR + 1, dtype=jnp.int32)
    valid_count = jnp.where(block_slot == 0, NEAR, valid_count)
    valid_count = jnp.where(block_slot == BLK_DEV - 1, 1, valid_count)
    return jnp.where(jnp.arange(NEAR, dtype=jnp.int32)[None, :] < valid_count[:, None], tiles_named, -1)


def draw_noise_var(key, part):
    key = jax.random.fold_in(key, 23)
    position = jnp.arange(NU, dtype=jnp.float32) / NU
    spread = jax.random.uniform(key, (NU,), jnp.float32, math.log(0.0001), math.log(0.0004))
    return jnp.exp(spread - math.log(3.0) * position)


def set_ends(drawn, rng, low, high):
    extent = drawn.shape
    spot = [jax.random.randint(jax.random.fold_in(rng, axis), (), 0, extent[axis]) for axis in range(len(extent))]
    drawn = drawn.at[tuple(spot)].set(low)
    longest = extent.index(max(extent))
    spot[longest] = (spot[longest] + 1) % extent[longest]
    return drawn.at[tuple(spot)].set(high)


def block_levels(key, dims, cuts, low, top_value):
    factor_of = 1.0
    for axis_at, blocks in cuts:
        heights = jax.random.uniform(jax.random.fold_in(jax.random.fold_in(key, 6), axis_at), (blocks,), jnp.float32, low / len(cuts), top_value / len(cuts))
        factor_of = factor_of * jnp.repeat(jnp.exp(heights), dims[axis_at] // blocks).reshape((-1,) + (1,) * (len(dims) - 1 - axis_at))
    return factor_of


def setup_inputs(seed: int = 0) -> dict:
    seeds = jax.random.split(jax.random.key(seed), 13)
    line_offset = jnp.clip(256.0 * jax.random.uniform(seeds[0], (LINES,), jnp.float32) ** block_levels(seeds[0], (LINES,), ((0, 64),), -0.2, 0.2), 0.0, 256.0)
    line_strength = jnp.clip(jnp.exp(math.log(5.0) - 3.218876 * jax.random.uniform(seeds[1], (LINES,), jnp.float32) ** block_levels(seeds[1], (LINES,), ((0, 64),), -0.2, 0.2)), 0.2, 5.0)
    lower_energy = jnp.clip(jnp.exp(math.log(2000.0) - 4.6051702 * jax.random.uniform(seeds[2], (LINES,), jnp.float32) ** block_levels(seeds[2], (LINES,), ((0, 64),), -0.2, 0.2)), 20.0, 2000.0)
    lorentz_width = jnp.clip(jnp.exp(math.log(60.0) - 2.7080502 * jax.random.uniform(seeds[3], (LINES,), jnp.float32) ** block_levels(seeds[3], (LINES,), ((0, 64),), -0.2, 0.2)), 4.0, 60.0)
    doppler_width = jnp.clip(jnp.exp(math.log(12.0) - 1.7917595 * jax.random.uniform(seeds[4], (LINES,), jnp.float32) ** block_levels(seeds[4], (LINES,), ((0, 64),), -0.2, 0.2)), 2.0, 12.0)
    line_species = set_ends(jax.random.randint(seeds[5], (LINES,), 0, SPECIES), jax.random.fold_in(seeds[5], 1), 0, SPECIES - 1).astype(jnp.int32)
    cutoff = draw_cutoff(jax.random.fold_in(seeds[12], 71), 0)
    layer_pressure = jnp.clip(jnp.exp(math.log(1.0) - 2.3025851 * jax.random.uniform(seeds[7], (LAYERS,), jnp.float32) ** block_levels(seeds[7], (LAYERS,), ((0, 4),), -0.2, 0.2)), 0.1, 1.0)
    layer_temp = jnp.clip(200.0 + 100.0 * jax.random.uniform(seeds[8], (LAYERS,), jnp.float32) ** block_levels(seeds[8], (LAYERS,), ((0, 4),), -0.2, 0.2), 200.0, 300.0)
    column_index = set_ends(jax.random.randint(seeds[9], (SOUND, LAYERS), 0, NCOL), jax.random.fold_in(seeds[9], 1), 0, NCOL - 1).astype(jnp.int32)
    column_table = jnp.clip(jnp.exp(jax.random.uniform(seeds[10], (SPECIES, NCOL), jnp.float32, math.log(0.03), math.log(0.3))), 0.03, 0.3)
    noise_var = draw_noise_var(jax.random.fold_in(seeds[12], 71), 0)
    return {"line_offset": line_offset, "line_strength": line_strength, "lower_energy": lower_energy, "lorentz_width": lorentz_width, "doppler_width": doppler_width, "line_species": line_species, "cutoff": cutoff, "layer_pressure": layer_pressure, "layer_temp": layer_temp, "column_index": column_index, "column_table": column_table, "noise_var": noise_var}


HIGH = lax.Precision.HIGHEST
LN_TWO = math.log(2.0)
C_TWO = 1.4388

def profile_widths(lorentz, gauss):
    full_width = (gauss ** 5 + 2.69269 * gauss ** 4 * lorentz + 2.42843 * gauss ** 3 * lorentz ** 2 + 4.47163 * gauss ** 2 * lorentz ** 3 + 0.07842 * gauss * lorentz ** 4 + lorentz ** 5) ** 0.2
    width_ratio = lorentz / full_width
    mixing = 1.36603 * width_ratio - 0.47719 * width_ratio ** 2 + 0.11116 * width_ratio ** 3
    return (full_width, mixing)

def profile_shape(distance, full_width, mixing):
    half_width = 0.5 * full_width
    lorentz_part = half_width / math.pi / (distance * distance + half_width * half_width)
    gauss_part = math.sqrt(4.0 * LN_TWO / math.pi) / full_width * jnp.exp(-4.0 * LN_TWO * distance * distance / (full_width * full_width))
    return mixing * lorentz_part + (1.0 - mixing) * gauss_part

def block_terms(offset, strength, energy, lwidth, dwidth, species, near_list, pressure, temper):
    lines_here = offset.shape[0]
    valid_count = jnp.maximum(jnp.sum((near_list >= 0).astype(jnp.int32)), 1)
    slot_index = jnp.arange(lines_here, dtype=jnp.int32) % valid_count
    home_tile = near_list[slot_index]
    temp_ratio = 296.0 / temper
    lorentz = lwidth[None, :] * (pressure * temp_ratio ** 0.75)[:, None]
    gauss = dwidth[None, :] * jnp.sqrt(temper / 296.0)[:, None]
    layer_strength = strength[None, :] * jnp.exp(-C_TWO * energy[None, :] * (1.0 / temper - 1.0 / 296.0)[:, None])
    species_rows = (species[None, :] == jnp.arange(3, dtype=jnp.float32)[:, None]).astype(jnp.float32)
    weights = layer_strength[:, None, :] * species_rows[None, :, :]
    tile_steps = (near_list[:, None] - home_tile[None, :]) * TILE
    grid_steps = tile_steps[:, :, None] + jnp.arange(TILE, dtype=jnp.int32)[None, None, :]
    distance = grid_steps.astype(jnp.float32) - offset[None, :, None]
    full_width, mixing = profile_widths(lorentz, gauss)
    profile = profile_shape(distance[:, None], full_width[None, :, :, None], mixing[None, :, :, None])
    tile_terms = jnp.einsum('lsk,jlkp->jlsp', weights, profile, precision=HIGH)
    return tile_terms.reshape(near_list.shape[0], -1)

def reference(line_offset, line_strength, lower_energy, lorentz_width, doppler_width, line_species, cutoff, layer_pressure, layer_temp, column_index, column_table, noise_var):

    def reshape_lines(values):
        return values.reshape(BLOCKS, LBLK)

    def single_block(packed):
        return block_terms(packed[0], packed[1], packed[2], packed[3], packed[4], packed[5], packed[6], layer_pressure, layer_temp)
    species_real = line_species.astype(jnp.float32)
    tile_terms = lax.map(single_block, (reshape_lines(line_offset), reshape_lines(line_strength), reshape_lines(lower_energy), reshape_lines(lorentz_width), reshape_lines(doppler_width), reshape_lines(species_real), cutoff))
    segment_ids = jnp.where(cutoff >= 0, cutoff, NT).reshape(-1).astype(jnp.int32)
    summed = jax.ops.segment_sum(tile_terms.reshape(BLOCKS * NEAR, -1), segment_ids, num_segments=NT + 1)[:NT]
    row_count = LAYERS * SPECIES
    cross = summed.reshape(NT, row_count, TILE).transpose(1, 0, 2).reshape(row_count, NU)
    chosen = (column_index[:, :, None] == jnp.arange(NCOL, dtype=jnp.int32)[None, None, :]).astype(jnp.float32)
    amounts = jnp.einsum('slc,pc->slp', chosen, column_table, precision=HIGH).reshape(SOUND, row_count)
    optical_depth = jnp.dot(amounts, cross, precision=HIGH)
    transmit = jnp.exp(-optical_depth)
    weight = transmit * transmit / noise_var[None, :] / NU

    def gram_block(sounding_pair):
        sounding_weight, sounding_amount = sounding_pair
        scaled = cross * sounding_weight[None, :]
        product = jnp.dot(scaled, cross.T, precision=HIGH)
        return product * sounding_amount[:, None] * sounding_amount[None, :]
    normals = lax.map(gram_block, (weight, amounts))
    return (transmit, normals)
```

```python
import math

import jax
import jax.numpy as jnp
from jax import lax
from jax.sharding import PartitionSpec as P

TILE = 256


HIGH = lax.Precision.HIGHEST
LN_TWO = math.log(2.0)
C_TWO = 1.4388


def passed_along(value, axis, by):
    peers = lax.axis_size(axis)
    pairs = [(i, i + by) for i in range(peers) if 0 <= i + by < peers]
    return lax.ppermute(value, axis, pairs)


def summed_over(value, axis, total, size, stride):
    members = [
        [base + stride * k for k in range(size)]
        for base in range(total)
        if (base // stride) % size == 0
    ]
    copies = jnp.broadcast_to(value[None], (size,) + value.shape)
    landed = lax.all_to_all(copies, axis, 0, 0, axis_index_groups=members, tiled=True)
    return jnp.sum(landed, axis=0)


def profile_widths(lorentz, gauss):
    full_width = (
        gauss**5
        + 2.69269 * gauss**4 * lorentz
        + 2.42843 * gauss**3 * lorentz**2
        + 4.47163 * gauss**2 * lorentz**3
        + 0.07842 * gauss * lorentz**4
        + lorentz**5
    ) ** 0.2
    width_ratio = lorentz / full_width
    mixing = 1.36603 * width_ratio - 0.47719 * width_ratio**2 + 0.11116 * width_ratio**3
    return (full_width, mixing)


def profile_shape(distance, full_width, mixing):
    half_width = 0.5 * full_width
    lorentz_part = half_width / math.pi / (distance * distance + half_width * half_width)
    gauss_part = (
        math.sqrt(4.0 * LN_TWO / math.pi)
        / full_width
        * jnp.exp(-4.0 * LN_TWO * distance * distance / (full_width * full_width))
    )
    return mixing * lorentz_part + (1.0 - mixing) * gauss_part


def block_terms(offset, strength, energy, lwidth, dwidth, species, near_list, pressure, temper):
    lines_here = offset.shape[0]
    valid_count = jnp.maximum(jnp.sum((near_list >= 0).astype(jnp.int32)), 1)
    slot_index = jnp.arange(lines_here, dtype=jnp.int32) % valid_count
    home_tile = jnp.sum(
        jnp.where(
            slot_index[None, :] == jnp.arange(near_list.shape[0], dtype=jnp.int32)[:, None],
            near_list[:, None],
            0,
        ),
        axis=0,
    )
    temp_ratio = 296.0 / temper
    lorentz = lwidth[None, :] * (pressure * temp_ratio**0.75)[:, None]
    gauss = dwidth[None, :] * jnp.sqrt(temper / 296.0)[:, None]
    layer_strength = strength[None, :] * jnp.exp(
        -C_TWO * energy[None, :] * (1.0 / temper - 1.0 / 296.0)[:, None]
    )
    species_rows = (species[None, :] == jnp.arange(3, dtype=jnp.float32)[:, None]).astype(
        jnp.float32
    )
    weights = layer_strength[:, None, :] * species_rows[None, :, :]
    tile_steps = (near_list[:, None] - home_tile[None, :]) * TILE
    grid_steps = tile_steps[:, :, None] + jnp.arange(TILE, dtype=jnp.int32)[None, None, :]
    distance = grid_steps.astype(jnp.float32) - offset[None, :, None]
    full_width, mixing = profile_widths(lorentz, gauss)
    profile = profile_shape(
        distance[:, None], full_width[None, :, :, None], mixing[None, :, :, None]
    )
    tile_terms = jnp.einsum("lsk,jlkp->jlsp", weights, profile, precision=HIGH)
    return tile_terms.reshape(near_list.shape[0], -1)


def body(
    line_offset,
    line_strength,
    lower_energy,
    lorentz_width,
    doppler_width,
    line_species,
    cutoff,
    layer_pressure,
    layer_temp,
    column_index,
    column_table,
    noise_var,
):
    tiles_dev = noise_var.shape[0] // TILE
    groups = lax.axis_size(("spec", "line"))
    total_tiles = tiles_dev * groups
    position = lax.axis_index(("spec", "line"))
    near_count = cutoff.shape[1]
    species_real = line_species.astype(jnp.float32)
    block_total = cutoff.shape[0]

    def by_block(values):
        return values.reshape(block_total, -1)

    mapped = jax.vmap(block_terms, in_axes=(0, 0, 0, 0, 0, 0, 0, None, None))
    result = mapped(
        by_block(line_offset),
        by_block(line_strength),
        by_block(lower_energy),
        by_block(lorentz_width),
        by_block(doppler_width),
        by_block(species_real),
        cutoff,
        layer_pressure,
        layer_temp,
    )
    tile_terms = result.reshape(block_total * near_count, -1)
    window_base = (position - 1) * tiles_dev
    wanted = window_base + jnp.arange(3 * tiles_dev, dtype=jnp.int32)
    selector = (cutoff.reshape(-1)[None, :] == wanted[:, None]).astype(jnp.float32)
    window = jnp.dot(selector, tile_terms, precision=HIGH)
    lower_part = window[:tiles_dev]
    middle = window[tiles_dev : 2 * tiles_dev]
    upper_part = window[2 * tiles_dev :]
    from_above = passed_along(lower_part, ("spec", "line"), -1)
    from_below = passed_along(upper_part, ("spec", "line"), 1)
    owned_tiles = middle + from_above + from_below
    row_count = owned_tiles.shape[1] // TILE
    cross_own = (
        owned_tiles.reshape(tiles_dev, row_count, TILE)
        .transpose(1, 0, 2)
        .reshape(row_count, tiles_dev * TILE)
    )
    table_size = column_table.shape[1]
    soundings = column_index.shape[0]
    chosen = (
        column_index[:, :, None] == jnp.arange(table_size, dtype=jnp.int32)[None, None, :]
    ).astype(jnp.float32)
    amounts = jnp.einsum("slc,pc->slp", chosen, column_table, precision=HIGH).reshape(soundings, -1)
    layer_slot = lax.axis_index("lay")
    own_amounts = lax.dynamic_slice_in_dim(amounts, layer_slot * row_count, row_count, 1)
    spectral = total_tiles * TILE
    cross_all = lax.all_gather(cross_own, "lay", axis=0, tiled=True)
    optical_depth = jnp.dot(amounts, cross_all, precision=HIGH)
    transmit = jnp.exp(-optical_depth)
    weight = transmit * transmit / noise_var[None, :] / spectral
    scaled = cross_own[None, :, :] * weight[:, None, :] * own_amounts[:, :, None]
    gram_block = jnp.einsum(
        "sav,bv->sab", scaled, cross_all, precision=HIGH
    )
    partial_normals = gram_block * amounts[:, None, :]
    flat = partial_normals.reshape(-1, 128)
    stride = 1
    while stride < groups:
        size = min(8, groups // stride)
        flat = summed_over(flat, ("spec", "line"), groups, size, stride)
        stride *= size
    normals = flat.reshape(partial_normals.shape)
    return (transmit, normals)


def solution(mesh):
    in_specs = (
        P(("spec", "line")),
        P(("spec", "line")),
        P(("spec", "line")),
        P(("spec", "line")),
        P(("spec", "line")),
        P(("spec", "line")),
        P(("spec", "line"), None),
        P("lay"),
        P("lay"),
        P(),
        P(),
        P(("spec", "line")),
    )
    out_specs = (P(None, ("spec", "line")), P(None, "lay", None))
    return jax.shard_map(body, mesh=mesh, in_specs=in_specs, out_specs=out_specs, check_vma=False)
```

```python
import functools
import math

import jax
import jax.numpy as jnp
from jax import lax
from jax.experimental import pallas as pl
from jax.experimental.pallas import tpu as pltpu
from jax.sharding import PartitionSpec as P

TILE = 256
LBLK = 128
NEAR = 4
SPECIES = 3
OWN_TILES = 4
GROUP = ("spec", "line")

HIGH = lax.Precision.HIGHEST
LN_TWO = math.log(2.0)
C_TWO = 1.4388
VMEM_BYTES = 40 * 1024 * 1024


def passed_along(value, by):
    peers = lax.axis_size(GROUP)
    pairs = [(i, i + by) for i in range(peers) if 0 <= i + by < peers]
    return lax.ppermute(value, GROUP, pairs)


def summed_over(copies, total, size, stride):
    members = [
        [base + stride * k for k in range(size)]
        for base in range(total)
        if (base // stride) % size == 0
    ]
    landed = lax.all_to_all(copies, GROUP, 0, 0, axis_index_groups=members, tiled=True)
    return jnp.sum(landed, axis=0)


def line_tables(near, temper_ref, press_ref, lines, home_ref, rate_ref, mix_ref, amp_ref):
    offset, strength, energy, lwidth, dwidth = lines
    shape = strength.shape
    count = jnp.sum((near >= 0).astype(jnp.int32), axis=1, keepdims=True)
    lane = lax.broadcasted_iota(jnp.int32, shape, 1)
    entry = jnp.where(
        count == 3,
        lax.rem(lane, 3),
        jnp.where(count == 4, lane & 3, jnp.where(count == 2, lane & 1, 0)),
    )
    home = near[:, NEAR - 1 : NEAR]
    for j in range(NEAR - 2, -1, -1):
        home = jnp.where(entry == j, near[:, j : j + 1], home)
    home_ref[...] = (home * TILE).astype(jnp.float32)
    for layer in range(2):
        temper = jnp.full(shape, temper_ref[layer], jnp.float32)
        ratio = 296.0 / temper
        lor = lwidth * (press_ref[layer] * jnp.exp(0.75 * jnp.log(ratio)))
        gau = dwidth * jnp.sqrt(temper / 296.0)
        line = strength * jnp.exp(-C_TWO * energy * (1.0 / temper - 1.0 / 296.0))
        g2 = gau * gau
        g4 = g2 * g2
        l2 = lor * lor
        l4 = l2 * l2
        total = (
            g4 * gau
            + 2.69269 * g4 * lor
            + 2.42843 * g2 * gau * l2
            + 4.47163 * g2 * lor * l2
            + 0.07842 * gau * l4
            + l4 * lor
        )
        width = jnp.exp(0.2 * jnp.log(total))
        inverse = 1.0 / width
        part = lor * inverse
        eta = part * (1.36603 + part * (-0.47719 + part * 0.11116))
        peak = eta * (2.0 / math.pi)
        rate_ref[layer] = -4.0 * inverse * inverse
        mix_ref[layer] = (1.0 - eta) * math.sqrt(4.0 * LN_TWO / math.pi) / peak
        amp_ref[layer] = line * peak * inverse


def pairs_kernel(
    outward,
    place_ref,
    near_ref,
    press_ref,
    temper_ref,
    near_hbm,
    offset_hbm,
    strength_hbm,
    energy_hbm,
    lwidth_hbm,
    dwidth_hbm,
    species_hbm,
    *rest,
):
    if outward:
        outs, scratch = rest[:2], rest[2:]
    else:
        index_ref, table_ref = rest[:2]
        outs, scratch = rest[2:5], rest[5:]
    (
        near_v,
        offset_v,
        strength_v,
        energy_v,
        lwidth_v,
        dwidth_v,
        species_v,
        sems,
        home_ref,
        rate_ref,
        mix_ref,
        amp_ref,
        acc_ref,
        list_ref,
        buf_a,
        buf_b,
    ) = scratch
    hbm = (near_hbm, offset_hbm, strength_hbm, energy_hbm, lwidth_hbm, dwidth_hbm, species_hbm)
    vmem = (near_v, offset_v, strength_v, energy_v, lwidth_v, dwidth_v, species_v)
    copies = [pltpu.make_async_copy(s, d, sems.at[i]) for i, (s, d) in enumerate(zip(hbm, vmem))]
    for copy in copies:
        copy.start()

    slots = acc_ref.shape[0] - 1
    blocks = near_v.shape[0]
    base = (place_ref[0] - 1) * OWN_TILES + (0 if outward else OWN_TILES)
    trash = slots * blocks
    list_ref[0] = jnp.int32(trash)
    found = jnp.int32(1)
    for b in range(blocks):
        for j in range(NEAR):
            tile = near_ref[b * NEAR + j]
            slot = tile - base
            valid = tile >= 0
            if outward:
                above = slot >= 2 * OWN_TILES
                valid &= (slot < OWN_TILES) | above
                slot = jnp.where(above, slot - OWN_TILES, slot)
            else:
                valid &= (slot >= 0) & (slot < OWN_TILES)
            list_ref[found] = slot * blocks + b
            found = found + valid.astype(jnp.int32)
    list_ref[found] = jnp.int32(trash)
    acc_ref[...] = jnp.zeros_like(acc_ref)

    for copy in copies:
        copy.wait()
    line_tables(
        near_v[...],
        temper_ref,
        press_ref,
        (offset_v[...], strength_v[...], energy_v[...], lwidth_v[...], dwidth_v[...]),
        home_ref,
        rate_ref,
        mix_ref,
        amp_ref,
    )

    rows = 16
    row = lax.broadcasted_iota(jnp.int32, (rows, LBLK), 0)
    part = row // SPECIES
    kind = row - part * SPECIES
    point = lax.broadcasted_iota(jnp.int32, (16, LBLK), 0).astype(jnp.float32)

    def decode(i):
        code = list_ref[i]
        return lax.div(code, blocks), lax.rem(code, blocks)

    def evaluate(i, buf):
        slot, b = decode(i)
        tile = slot + base
        if outward:
            tile = jnp.where(slot >= OWN_TILES, tile + OWN_TILES, tile)
        shift = ((tile * TILE).astype(jnp.float32) - home_ref[pl.ds(b, 1), :]) - offset_v[
            pl.ds(b, 1), :
        ]
        rate = [rate_ref[layer, pl.ds(b, 1), :] for layer in range(2)]
        mix = [mix_ref[layer, pl.ds(b, 1), :] for layer in range(2)]
        for k in range(0, TILE, 16):
            x = point + (shift + float(k))
            square = x * x
            for layer in range(2):
                q = square * rate[layer]
                value = 1.0 / (1.0 - q) + mix[layer] * jnp.exp2(q)
                high = value.astype(jnp.bfloat16)
                buf[layer, k : k + 16, :LBLK] = high
                buf[layer, k : k + 16, LBLK:] = (value - high.astype(jnp.float32)).astype(
                    jnp.bfloat16
                )

    def reduce(i, buf):
        slot, b = decode(i)
        same = kind == species_v[pl.ds(b, 1), :]
        for layer in range(2):
            amp = jnp.broadcast_to(amp_ref[layer, pl.ds(b, 1), :], (rows, LBLK))
            one = amp.astype(jnp.bfloat16).astype(jnp.float32)
            left = amp - one
            two = left.astype(jnp.bfloat16).astype(jnp.float32)
            split = jnp.where(
                part == 0, one, jnp.where(part == 1, two, jnp.where(part == 2, left - two, 0.0))
            )
            weights = jnp.where(same, split, 0.0).astype(jnp.bfloat16)
            weights = jnp.concatenate([weights, weights], axis=1)
            acc_ref[slot, layer] += lax.dot_general(
                weights,
                buf[layer],
                (((1,), (1,)), ((), ())),
                preferred_element_type=jnp.float32,
            )

    def step(i, carry):
        evaluate(2 * i + 1, buf_a)
        reduce(2 * i, buf_b)
        evaluate(2 * i + 2, buf_b)
        reduce(2 * i + 1, buf_a)
        return carry

    turns = lax.div(found, 2)
    lax.fori_loop(0, turns, step, 0)
    reduce(2 * turns, buf_b)

    for slot in range(slots):
        out = outs[slot // OWN_TILES]
        at = (slot % OWN_TILES) * TILE
        for layer in range(2):
            sums = acc_ref[slot, layer]
            out[SPECIES * layer : SPECIES * (layer + 1), at : at + TILE] = (
                sums[:SPECIES] + sums[SPECIES : 2 * SPECIES] + sums[2 * SPECIES : 3 * SPECIES]
            )

    if not outward:
        amount_tables(place_ref[1], index_ref, table_ref, outs[1], outs[2])


def amount_tables(lay, index_ref, table_ref, amounts_ref, factor_ref):
    sounds, layers = index_ref.shape
    entries = table_ref.shape[1]
    columns = layers * SPECIES
    lane = lax.broadcasted_iota(jnp.int32, (sounds, columns), 1)
    entry = lax.broadcasted_iota(jnp.int32, (sounds, entries), 1)
    amounts = jnp.zeros((sounds, columns), jnp.float32)
    for layer in range(layers):
        hit = entry == index_ref[:, layer : layer + 1]
        for kind in range(SPECIES):
            column = jnp.sum(
                jnp.where(hit, table_ref[kind : kind + 1, :], 0.0), axis=1, keepdims=True
            )
            amounts = jnp.where(lane == SPECIES * layer + kind, column, amounts)
    amounts_ref[...] = amounts
    own = factor_ref.shape[0]
    for a in range(own):
        column = jnp.sum(
            jnp.where(lane == own * lay + a, amounts, 0.0), axis=1, keepdims=True
        )
        factor_ref[a] = column * amounts


def pair_sums(outward, place, near, press, temper, lines, index=None, table=None):
    blocks = near.shape[0]
    row_count = 2 * SPECIES
    width = OWN_TILES * TILE
    smem = pl.BlockSpec(memory_space=pltpu.SMEM)
    vmem = pl.BlockSpec(memory_space=pltpu.VMEM)
    hbm = pl.BlockSpec(memory_space=pl.ANY)
    block_shape = (blocks, LBLK)
    f32 = functools.partial(pltpu.VMEM, dtype=jnp.float32)
    slots = (2 if outward else 1) * OWN_TILES
    sums = jax.ShapeDtypeStruct((row_count, width), jnp.float32)
    in_specs = [smem] * 4 + [hbm] * 7
    args = [place, near.reshape(-1), press, temper, near] + [v.reshape(block_shape) for v in lines]
    if outward:
        out_shape = (sums, sums)
    else:
        sounds, layers = index.shape
        columns = layers * SPECIES
        out_shape = (
            sums,
            jax.ShapeDtypeStruct((sounds, columns), jnp.float32),
            jax.ShapeDtypeStruct((row_count, sounds, columns), jnp.float32),
        )
        in_specs += [vmem] * 2
        args += [index, table]
    return pl.pallas_call(
        functools.partial(pairs_kernel, outward),
        out_shape=out_shape,
        in_specs=in_specs,
        out_specs=[vmem] * len(out_shape),
        scratch_shapes=[pltpu.VMEM(near.shape, jnp.int32)]
        + [f32(block_shape)] * 5
        + [
            pltpu.VMEM(block_shape, jnp.int32),
            pltpu.SemaphoreType.DMA((7,)),
            f32(block_shape),
            f32((2,) + block_shape),
            f32((2,) + block_shape),
            f32((2,) + block_shape),
            f32((slots + 1, 2, 16, TILE)),
            pltpu.SMEM((blocks * NEAR + 2,), jnp.int32),
            pltpu.VMEM((2, TILE, 2 * LBLK), jnp.bfloat16),
            pltpu.VMEM((2, TILE, 2 * LBLK), jnp.bfloat16),
        ],
        compiler_params=pltpu.CompilerParams(vmem_limit_bytes=VMEM_BYTES),
        cost_estimate=pl.CostEstimate(
            flops=2_000_000_000 * (2 if outward else 1), bytes_accessed=200_000, transcendentals=0
        ),
        name="outward_pairs" if outward else "own_pairs",
    )(*args)


def gram_kernel(points, all_ref, own_ref, amounts_ref, factor_ref, noise_ref, transmit_ref, out_ref):
    cross = all_ref[...]
    depth = jnp.dot(
        amounts_ref[...], cross, precision=HIGH, preferred_element_type=jnp.float32
    )
    passed = jnp.exp(-depth)
    transmit_ref[...] = passed
    weight = passed * passed / noise_ref[...] * (1.0 / points)
    own = own_ref.shape[0]
    for a in range(own):
        scaled = weight * own_ref[a : a + 1, :]
        gram = lax.dot_general(
            scaled,
            cross,
            (((1,), (1,)), ((), ())),
            precision=HIGH,
            preferred_element_type=jnp.float32,
        )
        out_ref[a] = gram * factor_ref[a]


def gram_parts(points, cross_all, cross_own, amounts, factor, noise):
    sounds, columns = amounts.shape
    width = noise.shape[0]
    vmem = pl.BlockSpec(memory_space=pltpu.VMEM)
    return pl.pallas_call(
        functools.partial(gram_kernel, points),
        out_shape=(
            jax.ShapeDtypeStruct((sounds, width), jnp.float32),
            jax.ShapeDtypeStruct(factor.shape, jnp.float32),
        ),
        in_specs=[vmem] * 5,
        out_specs=[vmem] * 2,
        compiler_params=pltpu.CompilerParams(vmem_limit_bytes=VMEM_BYTES),
        name="gram_parts",
    )(cross_all, cross_own, amounts, factor, noise.reshape(1, -1))


def body(
    line_offset,
    line_strength,
    lower_energy,
    lorentz_width,
    doppler_width,
    line_species,
    cutoff,
    layer_pressure,
    layer_temp,
    column_index,
    column_table,
    noise_var,
):
    groups = lax.axis_size(GROUP)
    place = jnp.stack([lax.axis_index(GROUP), lax.axis_index("lay")]).astype(jnp.int32)
    lines = (
        line_offset,
        line_strength,
        lower_energy,
        lorentz_width,
        doppler_width,
        line_species,
    )
    shared = (place, cutoff, layer_pressure, layer_temp, lines)
    lower_part, upper_part = pair_sums(True, *shared)
    from_above = passed_along(lower_part, -1)
    from_below = passed_along(upper_part, 1)
    middle, amounts, factor = pair_sums(False, *shared, column_index, column_table)
    cross_own = middle + from_above + from_below
    cross_all = lax.all_gather(cross_own, "lay", axis=0, tiled=True)
    points = noise_var.shape[0] * groups
    transmit, partial = gram_parts(points, cross_all, cross_own, amounts, factor, noise_var)
    flat = partial.reshape(-1, 128)
    stride = 1
    while stride < groups:
        size = min(8, groups // stride)
        copies = jnp.broadcast_to(flat[None], (size,) + flat.shape)
        flat = summed_over(copies, groups, size, stride)
        stride *= size
    normals = flat.reshape(partial.shape).transpose(1, 0, 2)
    return (transmit, normals)


def solution(mesh):
    in_specs = (
        P(GROUP),
        P(GROUP),
        P(GROUP),
        P(GROUP),
        P(GROUP),
        P(GROUP),
        P(GROUP, None),
        P("lay"),
        P("lay"),
        P(),
        P(),
        P(GROUP),
    )
    out_specs = (P(None, GROUP), P(None, "lay", None))
    return jax.shard_map(body, mesh=mesh, in_specs=in_specs, out_specs=out_specs, check_vma=False)
```

```python
import functools
import math

import jax
import jax.numpy as jnp
from jax import lax
from jax.experimental import pallas as pl
from jax.experimental.pallas import tpu as pltpu
from jax.sharding import PartitionSpec as P

TILE = 256
LBLK = 128
NEAR = 4
SPECIES = 3
OWN_TILES = 4
HOME_BATCH = 4
AWAY_BATCH = 2
GROUP = ("spec", "line")

HIGH = lax.Precision.HIGHEST
LN_TWO = math.log(2.0)
C_TWO = 1.4388
VMEM_BYTES = 40 * 1024 * 1024


def exchanged(value, start):
    peers = lax.axis_size(GROUP)
    pairs = [(i, i + 1) for i in range(start, peers - 1, 2)]
    return lax.ppermute(value, GROUP, pairs + [(j, i) for i, j in pairs])


def summed_over(copies, total, size, stride):
    members = [
        [base + stride * k for k in range(size)]
        for base in range(total)
        if (base // stride) % size == 0
    ]
    landed = lax.all_to_all(copies, GROUP, 0, 0, axis_index_groups=members, tiled=True)
    return jnp.sum(landed, axis=0)


def line_tables(press, temper, strength, energy, lwidth, dwidth, rate_ref, mix_ref, amp_ref):
    shape = strength.shape
    for layer in range(2):
        temp = jnp.broadcast_to(temper[:, layer : layer + 1], shape)
        pressure = jnp.broadcast_to(press[:, layer : layer + 1], shape)
        ratio = 296.0 / temp
        lor = lwidth * (pressure * jnp.exp(0.75 * jnp.log(ratio)))
        gau = dwidth * jnp.sqrt(temp / 296.0)
        line = strength * jnp.exp(-C_TWO * energy * (1.0 / temp - 1.0 / 296.0))
        g2 = gau * gau
        g4 = g2 * g2
        l2 = lor * lor
        l4 = l2 * l2
        total = (
            g4 * gau
            + 2.69269 * g4 * lor
            + 2.42843 * g2 * gau * l2
            + 4.47163 * g2 * lor * l2
            + 0.07842 * gau * l4
            + l4 * lor
        )
        width = jnp.exp(0.2 * jnp.log(total))
        inverse = 1.0 / width
        part = lor * inverse
        eta = part * (1.36603 + part * (-0.47719 + part * 0.11116))
        peak = eta * (2.0 / math.pi)
        rate_ref[layer] = -4.0 * inverse * inverse
        mix_ref[layer] = (1.0 - eta) * math.sqrt(4.0 * LN_TWO / math.pi) / peak
        amp_ref[layer] = line * peak * inverse


def own_place():
    return lax.axis_index(GROUP), lax.axis_index("lay")


def pairs_kernel(*refs):
    hbm, outs, scratch = refs[:9], refs[9:12], refs[12:]
    vmem, sems = scratch[:9], scratch[9]
    near, press_v, temper_v, offset_v, strength_v, energy_v, lwidth_v, dwidth_v, species_v = vmem
    rate_ref, mix_ref, amp_ref, point_ref, list_ref = scratch[10:15]
    home_acc, away_acc = scratch[15:17], scratch[17:19]
    home_bufs = scratch[19 : 19 + 2 * HOME_BATCH]
    away_bufs = home_bufs[: 2 * AWAY_BATCH]
    copies = [pltpu.make_async_copy(s, d, sems.at[i]) for i, (s, d) in enumerate(zip(hbm, vmem))]
    for copy in copies:
        copy.start()
    for acc in home_acc + away_acc:
        acc[...] = jnp.zeros_like(acc)
    point_ref[...] = lax.broadcasted_iota(jnp.int32, point_ref.shape, 0).astype(jnp.float32)

    slots = home_acc[0].shape[0] - 1
    blocks = near.shape[1]
    group = own_place()[0]
    base = (group - 1) * OWN_TILES
    copies[0].wait()
    pad = 2 * AWAY_BATCH
    for k in range(pad):
        list_ref[k] = jnp.int32(0)
    found = jnp.int32(pad)
    for b in range(blocks):
        for j in range(1, NEAR):
            list_ref[found] = jnp.int32(NEAR * b + j)
            found = found + (near[j, b] >= 0).astype(jnp.int32)
    for k in range(2 * pad):
        list_ref[found + k] = jnp.int32(0)

    for copy in copies[1:]:
        copy.wait()
    line_tables(
        press_v[...],
        temper_v[...],
        strength_v[...],
        energy_v[...],
        lwidth_v[...],
        dwidth_v[...],
        rate_ref,
        mix_ref,
        amp_ref,
    )

    lane = lax.broadcasted_iota(jnp.int32, (1, LBLK), 1)
    lane_three = lax.rem(lane, 3)
    home_row = lax.broadcasted_iota(jnp.int32, (NEAR * 8, LBLK), 0)
    home_part = home_row & 7
    home_rest = home_part >= SPECIES
    home_key = jnp.where(
        home_part < 2 * SPECIES, home_row - jnp.where(home_rest, SPECIES, 0), -1
    )
    away_key = lax.broadcasted_iota(jnp.int32, (NEAR * 4, LBLK), 0)
    upper_half = lax.broadcasted_iota(jnp.int32, (8, TILE), 0) >= 4

    def entries(b):
        tiles = [near[j, b] for j in range(NEAR)]
        count = jnp.int32(1)
        for j in range(1, NEAR):
            count = count + (tiles[j] >= 0).astype(jnp.int32)
        own = jnp.where(count == 3, lane_three, lane & jnp.where(count == 4, 3, count - 1))
        return tiles, count, own

    def rotated(own, count, r):
        entry = own + r
        return jnp.where(entry >= count, entry - count, entry)

    def chosen(entry, tiles):
        tile = jnp.where(entry == 0, tiles[0], tiles[NEAR - 1])
        for j in range(1, NEAR - 1):
            tile = jnp.where(entry == j, tiles[j], tile)
        return tile

    def evaluate(b, shift, buf, at, split):
        shape = (16, LBLK)
        shift = jnp.broadcast_to(shift, shape)
        rate = [jnp.broadcast_to(rate_ref[layer, pl.ds(b, 1), :], shape) for layer in range(2)]
        mix = [jnp.broadcast_to(mix_ref[layer, pl.ds(b, 1), :], shape) for layer in range(2)]
        for k in range(0, TILE, 16):
            x = point_ref[k : k + 16, :] + shift
            square = x * x
            for layer in range(2):
                q = square * rate[layer]
                value = 1.0 / (1.0 - q) + mix[layer] * jnp.exp2(q)
                high = value.astype(jnp.bfloat16)
                buf[layer, k : k + 16, at : at + LBLK] = high
                if split:
                    buf[layer, k : k + 16, LBLK:] = (value - high.astype(jnp.float32)).astype(
                        jnp.bfloat16
                    )

    def times(left, right):
        return lax.dot_general(
            left, right, (((1,), (1,)), ((), ())), preferred_element_type=jnp.float32
        )

    def slot_of(tile, live):
        return jnp.where(live & (tile >= 0), tile - base, slots)

    def home_evaluate(b, buf):
        evaluate(b, -offset_v[pl.ds(b, 1), :], buf, 0, True)

    def home_reduce(b, buf):
        live = b >= 0
        b = jnp.maximum(b, 0)
        tiles, _, own = entries(b)
        hit = home_key == own * 8 + species_v[pl.ds(b, 1), :]
        for layer in range(2):
            amp = jnp.broadcast_to(amp_ref[layer, pl.ds(b, 1), :], home_row.shape)
            high = amp.astype(jnp.bfloat16).astype(jnp.float32)
            part = jnp.where(home_rest, amp - high, high)
            left = jnp.where(hit, part, 0.0).astype(jnp.bfloat16)
            sums = times(jnp.concatenate([left, left], axis=1), buf[layer])
            for j in range(NEAR):
                home_acc[layer][slot_of(tiles[j], live)] += sums[8 * j : 8 * j + 8]

    def decode(i):
        code = list_ref[i]
        return lax.shift_right_logical(code, 2), code & 3

    def away_evaluate(i, buf):
        for k in range(2):
            b, r = decode(2 * i + k)
            tiles, count, own = entries(b)
            apart = chosen(rotated(own, count, r), tiles) - chosen(own, tiles)
            shift = (apart * TILE).astype(jnp.float32) - offset_v[pl.ds(b, 1), :]
            evaluate(b, shift, buf, k * LBLK, False)

    def away_reduce(i, buf):
        items = []
        for k in range(2):
            b, r = decode(2 * i + k)
            tiles, count, own = entries(b)
            key = rotated(own, count, r) * 4 + species_v[pl.ds(b, 1), :]
            items.append((b, away_key == key, [slot_of(tile, r > 0) for tile in tiles]))
        empty = jnp.zeros(away_key.shape, jnp.bfloat16)
        for layer in range(2):
            left = [
                jnp.where(
                    hit, jnp.broadcast_to(amp_ref[layer, pl.ds(b, 1), :], away_key.shape), 0.0
                ).astype(jnp.bfloat16)
                for b, hit, _ in items
            ]
            stacked = jnp.concatenate(
                [
                    jnp.concatenate([left[0], empty], axis=1),
                    jnp.concatenate([empty, left[1]], axis=1),
                ],
                axis=0,
            )
            sums = times(stacked, buf[layer])
            for k, (_, _, slot) in enumerate(items):
                for j in range(NEAR):
                    at = 16 * k + 8 * (j // 2)
                    part = sums[at : at + 8]
                    part = jnp.where(upper_half, part, 0.0) if j % 2 else jnp.where(upper_half, 0.0, part)
                    away_acc[layer][slot[j]] += part

    def alternate(batch, bufs, evaluate_one, reduce_one, turns):
        def step(i, carry):
            at = 2 * batch * i
            for k in range(batch):
                evaluate_one(at + k, bufs[k])
            for k in range(batch):
                reduce_one(at - batch + k, bufs[batch + k])
            for k in range(batch):
                evaluate_one(at + batch + k, bufs[batch + k])
            for k in range(batch):
                reduce_one(at + k, bufs[k])
            return carry

        lax.fori_loop(0, turns, step, 0)
        for k in range(batch):
            reduce_one(2 * batch * turns - batch + k, bufs[batch + k])

    alternate(
        HOME_BATCH, home_bufs, home_evaluate, home_reduce, jnp.int32(blocks // (2 * HOME_BATCH))
    )
    span = 4 * AWAY_BATCH
    alternate(
        AWAY_BATCH,
        away_bufs,
        lambda i, buf: away_evaluate(i + AWAY_BATCH, buf),
        lambda i, buf: away_reduce(i + AWAY_BATCH, buf),
        lax.div(found - pad + span - 1, span),
    )

    even = (group & 1) == 0
    for slot in range(OWN_TILES):
        at = slot * TILE
        for layer in range(2):
            parts = []
            for third in range(3):
                home = home_acc[layer][third * OWN_TILES + slot]
                away = away_acc[layer][third * OWN_TILES + slot]
                parts.append(
                    home[:SPECIES]
                    + home[SPECIES : 2 * SPECIES]
                    + (away[:SPECIES] + away[4 : 4 + SPECIES])
                )
            where = (slice(SPECIES * layer, SPECIES * (layer + 1)), slice(at, at + TILE))
            outs[0][where] = jnp.where(even, parts[2], parts[0])
            outs[1][where] = parts[1]
            outs[2][where] = jnp.where(even, parts[0], parts[2])


def pair_sums(near, press, temper, lines):
    blocks = near.shape[1]
    row_count = 2 * SPECIES
    vmem = pl.BlockSpec(memory_space=pltpu.VMEM)
    hbm = pl.BlockSpec(memory_space=pltpu.HBM)
    block_shape = (blocks, LBLK)
    f32 = functools.partial(pltpu.VMEM, dtype=jnp.float32)
    sums = jax.ShapeDtypeStruct((row_count, OWN_TILES * TILE), jnp.float32)
    return pl.pallas_call(
        pairs_kernel,
        out_shape=(sums,) * 3,
        in_specs=[hbm] * 9,
        out_specs=[vmem] * 3,
        scratch_shapes=[pltpu.SMEM(near.shape, jnp.int32), f32((1, 2)), f32((1, 2))]
        + [f32(block_shape)] * 5
        + [
            pltpu.VMEM(block_shape, jnp.int32),
            pltpu.SemaphoreType.DMA((9,)),
            f32((2,) + block_shape),
            f32((2,) + block_shape),
            f32((2,) + block_shape),
            f32((TILE, LBLK)),
            pltpu.SMEM((blocks * (NEAR - 1) + 6 * AWAY_BATCH,), jnp.int32),
        ]
        + [f32((3 * OWN_TILES + 1, 8, TILE))] * 4
        + [pltpu.VMEM((2, TILE, 2 * LBLK), jnp.bfloat16)] * (2 * HOME_BATCH),
        name="pair_sums",
    )(near, press.reshape(1, 2), temper.reshape(1, 2), *[v.reshape(block_shape) for v in lines])


def amounts_kernel(
    points, index_ref, table_ref, noise_ref, sums_ref, amounts_ref, factor_ref, scale_ref, out_ref
):
    out_ref[...] = sums_ref[...]
    scale_ref[...] = (1.0 / points) / noise_ref[...]
    layers, sounds = index_ref.shape
    kinds, entries = table_ref.shape
    entry = lax.broadcasted_iota(jnp.int32, (entries, sounds), 0)
    for layer in range(layers):
        hit = (entry == index_ref[layer : layer + 1, :]).astype(jnp.float32)
        amounts_ref[kinds * layer : kinds * (layer + 1), :] = jnp.dot(
            table_ref[...], hit, precision=HIGH, preferred_element_type=jnp.float32
        )
    amounts = amounts_ref[...]
    own = factor_ref.shape[0]
    first = own * own_place()[1]
    for a in range(own):
        factor_ref[a] = amounts * amounts_ref[pl.ds(first + a, 1), :]


def amount_tables(points, index, table, noise, sums):
    layers, sounds = index.shape
    columns = layers * SPECIES
    vmem = pl.BlockSpec(memory_space=pltpu.VMEM)
    return pl.pallas_call(
        functools.partial(amounts_kernel, points),
        out_shape=(
            jax.ShapeDtypeStruct((columns, sounds), jnp.float32),
            jax.ShapeDtypeStruct((2 * SPECIES, columns, sounds), jnp.float32),
            jax.ShapeDtypeStruct((1, noise.shape[0]), jnp.float32),
            jax.ShapeDtypeStruct(sums.shape, jnp.float32),
        ),
        in_specs=[vmem] * 4,
        out_specs=[vmem] * 4,
        compiler_params=pltpu.CompilerParams(vmem_limit_bytes=VMEM_BYTES),
        cost_estimate=pl.CostEstimate(flops=2_000_000, bytes_accessed=100_000, transcendentals=0),
        name="amount_tables",
    )(index, table, noise.reshape(1, -1), sums)


def gram_kernel(all_ref, amounts_ref, factor_ref, scale_ref, transmit_ref, out_ref):
    lays, own = all_ref.shape[:2]
    cross = jnp.concatenate([all_ref[i] for i in range(lays)], axis=0)
    depth = lax.dot_general(
        amounts_ref[...],
        cross,
        (((0,), (0,)), ((), ())),
        precision=HIGH,
        preferred_element_type=jnp.float32,
    )
    passed = jnp.exp(-depth)
    transmit_ref[...] = passed
    weight = passed * passed * scale_ref[...]
    lay = own_place()[1]
    for a in range(own):
        scaled = weight * all_ref[lay, a : a + 1, :]
        gram = lax.dot_general(
            cross,
            scaled,
            (((1,), (1,)), ((), ())),
            precision=HIGH,
            preferred_element_type=jnp.float32,
        )
        out_ref[a] = gram * factor_ref[a]


def gram_parts(cross_all, amounts, factor, scale):
    sounds = amounts.shape[1]
    width = scale.shape[1]
    vmem = pl.BlockSpec(memory_space=pltpu.VMEM)
    return pl.pallas_call(
        gram_kernel,
        out_shape=(
            jax.ShapeDtypeStruct((sounds, width), jnp.float32),
            jax.ShapeDtypeStruct(factor.shape, jnp.float32),
        ),
        in_specs=[vmem] * 4,
        out_specs=[vmem] * 2,
        compiler_params=pltpu.CompilerParams(vmem_limit_bytes=VMEM_BYTES),
        name="gram_parts",
    )(cross_all, amounts, factor, scale)


def body(
    line_offset,
    line_strength,
    lower_energy,
    lorentz_width,
    doppler_width,
    line_species,
    cutoff,
    layer_pressure,
    layer_temp,
    column_index,
    column_table,
    noise_var,
):
    groups = lax.axis_size(GROUP)
    lines = (
        line_offset,
        line_strength,
        lower_energy,
        lorentz_width,
        doppler_width,
        line_species,
    )
    first, middle, second = pair_sums(cutoff.T, layer_pressure, layer_temp, lines)
    landed = [exchanged(first, 0), exchanged(second, 1)]
    points = noise_var.shape[0] * groups
    amounts, factor, scale, middle = amount_tables(
        points, column_index.T, column_table, noise_var, middle
    )
    cross_own = middle + landed[0] + landed[1]
    cross_all = lax.all_gather(cross_own, "lay", axis=0)
    transmit, partial = gram_parts(cross_all, amounts, factor, scale)
    flat = partial.reshape(-1, 128)
    stride = 1
    while stride < groups:
        size = min(8, groups // stride)
        copies = jnp.broadcast_to(flat[None], (size,) + flat.shape)
        flat = summed_over(copies, groups, size, stride)
        stride *= size
    normals = flat.reshape(partial.shape).transpose(2, 0, 1)
    return (transmit, normals)


def solution(mesh):
    in_specs = (
        P(GROUP),
        P(GROUP),
        P(GROUP),
        P(GROUP),
        P(GROUP),
        P(GROUP),
        P(GROUP, None),
        P("lay"),
        P("lay"),
        P(),
        P(),
        P(GROUP),
    )
    out_specs = (P(None, GROUP), P(None, "lay", None))
    return jax.shard_map(body, mesh=mesh, in_specs=in_specs, out_specs=out_specs, check_vma=False)
```

```python
import functools
import math

import jax
import jax.numpy as jnp
from jax import lax
from jax.experimental import pallas as pl
from jax.experimental.pallas import tpu as pltpu
from jax.sharding import PartitionSpec as P

TILE = 256
LBLK = 128
NEAR = 4
SPECIES = 3
OWN_TILES = 4
HOME_BATCH = 16
AWAY_BATCH = 8
TAIL_BATCH = 4
GROUP = ("spec", "line")

HIGH = lax.Precision.HIGHEST
LN_TWO = math.log(2.0)
C_TWO = 1.4388
VMEM_BYTES = 40 * 1024 * 1024


def exchanged(value):
    pairs = [(i, i ^ 1) for i in range(lax.axis_size(GROUP))]
    return lax.ppermute(value, GROUP, pairs)


def all_layers(own, other, groups):
    lays = lax.axis_size("lay")
    members = [
        [lays * (d % groups) + i for d in (odd, odd + 1) for i in range(lays)]
        for odd in range(1, groups, 2)
    ]
    is_odd = (lax.axis_index(GROUP) & 1) == 1
    halves = jnp.stack([jnp.where(is_odd, own, other), jnp.where(is_odd, other, own)])
    copies = jnp.broadcast_to(halves[:, None], (2, lays) + own.shape)
    landed = lax.all_to_all(
        copies.reshape((2 * lays,) + own.shape),
        GROUP + ("lay",),
        0,
        0,
        axis_index_groups=members,
        tiled=True,
    )
    return landed.reshape(copies.shape)


def summed_over(copies, total, size, stride):
    members = [
        [base + stride * k for k in range(size)]
        for base in range(total)
        if (base // stride) % size == 0
    ]
    landed = lax.all_to_all(copies, GROUP, 0, 0, axis_index_groups=members, tiled=True)
    return jnp.sum(landed, axis=0)


def line_tables(press, temper, strength, energy, lwidth, dwidth, rate_ref, mix_ref, amp_ref):
    shape = strength.shape
    for layer in range(2):
        temp = jnp.broadcast_to(temper[:, layer : layer + 1], shape)
        pressure = jnp.broadcast_to(press[:, layer : layer + 1], shape)
        ratio = 296.0 / temp
        lor = lwidth * (pressure * jnp.exp(0.75 * jnp.log(ratio)))
        gau = dwidth * jnp.sqrt(temp / 296.0)
        line = strength * jnp.exp(-C_TWO * energy * (1.0 / temp - 1.0 / 296.0))
        g2 = gau * gau
        g4 = g2 * g2
        l2 = lor * lor
        l4 = l2 * l2
        total = (
            g4 * gau
            + 2.69269 * g4 * lor
            + 2.42843 * g2 * gau * l2
            + 4.47163 * g2 * lor * l2
            + 0.07842 * gau * l4
            + l4 * lor
        )
        width = jnp.exp(0.2 * jnp.log(total))
        inverse = 1.0 / width
        part = lor * inverse
        eta = part * (1.36603 + part * (-0.47719 + part * 0.11116))
        peak = eta * (2.0 / math.pi)
        rate_ref[layer] = -4.0 * inverse * inverse
        mix_ref[layer] = (1.0 - eta) * math.sqrt(4.0 * LN_TWO / math.pi) / peak
        amp_ref[layer] = line * peak * inverse


def own_place():
    return lax.axis_index(GROUP), lax.axis_index("lay")


def pairs_kernel(*refs):
    hbm, outs, scratch = refs[:9], refs[9:12], refs[12:]
    vmem, sems = scratch[:9], scratch[9]
    near, press_v, temper_v, offset_v, strength_v, energy_v, lwidth_v, dwidth_v, species_v = vmem
    rate_ref, mix_ref, amp_ref, point_ref, list_ref = scratch[10:15]
    home_acc, away_acc = scratch[15:17], scratch[17:19]
    copies = [pltpu.make_async_copy(s, d, sems.at[i]) for i, (s, d) in enumerate(zip(hbm, vmem))]
    for copy in copies:
        copy.start()
    for acc in home_acc + away_acc:
        acc[...] = jnp.zeros_like(acc)
    point_ref[...] = lax.broadcasted_iota(jnp.int32, point_ref.shape, 0).astype(jnp.float32)

    slots = home_acc[0].shape[0] - 1
    blocks = near.shape[1]
    group = own_place()[0]
    base = (group - 1) * OWN_TILES
    copies[0].wait()
    found = jnp.int32(0)
    for b in range(blocks):
        for j in range(1, NEAR):
            list_ref[found] = jnp.int32(NEAR * b + j)
            found = found + (near[j, b] >= 0).astype(jnp.int32)
    for k in range(2 * TAIL_BATCH):
        list_ref[found + k] = jnp.int32(0)

    for copy in copies[1:]:
        copy.wait()
    line_tables(
        press_v[...],
        temper_v[...],
        strength_v[...],
        energy_v[...],
        lwidth_v[...],
        dwidth_v[...],
        rate_ref,
        mix_ref,
        amp_ref,
    )

    lane = lax.broadcasted_iota(jnp.int32, (1, LBLK), 1)
    lane_three = lax.rem(lane, 3)
    home_row = lax.broadcasted_iota(jnp.int32, (NEAR * 8, LBLK), 0)
    home_part = home_row & 7
    home_rest = home_part >= SPECIES
    home_key = jnp.where(
        home_part < 2 * SPECIES, home_row - jnp.where(home_rest, SPECIES, 0), -1
    )
    away_key = lax.broadcasted_iota(jnp.int32, (NEAR * 4, LBLK), 0)
    upper_half = lax.broadcasted_iota(jnp.int32, (8, TILE), 0) >= 4

    def entries(b):
        tiles = [near[j, b] for j in range(NEAR)]
        count = jnp.int32(1)
        for j in range(1, NEAR):
            count = count + (tiles[j] >= 0).astype(jnp.int32)
        own = jnp.where(count == 3, lane_three, lane & jnp.where(count == 4, 3, count - 1))
        return tiles, count, own

    def rotated(own, count, r):
        entry = own + r
        return jnp.where(entry >= count, entry - count, entry)

    def chosen(entry, tiles):
        tile = jnp.where(entry == 0, tiles[0], tiles[NEAR - 1])
        for j in range(1, NEAR - 1):
            tile = jnp.where(entry == j, tiles[j], tile)
        return tile

    def evaluate(b, shift, split):
        shape = (16, LBLK)
        shift = jnp.broadcast_to(shift, shape)
        rate = [jnp.broadcast_to(rate_ref[layer, pl.ds(b, 1), :], shape) for layer in range(2)]
        mix = [jnp.broadcast_to(mix_ref[layer, pl.ds(b, 1), :], shape) for layer in range(2)]
        parts = [[], []]
        for k in range(0, TILE, 16):
            x = point_ref[k : k + 16, :] + shift
            square = x * x
            for layer in range(2):
                q = square * rate[layer]
                value = 1.0 / (1.0 - q) + mix[layer] * jnp.exp2(q)
                high = value.astype(jnp.bfloat16)
                if split:
                    low = (value - high.astype(jnp.float32)).astype(jnp.bfloat16)
                    high = jnp.concatenate([high, low], axis=1)
                parts[layer].append(high)
        return [jnp.concatenate(p, axis=0) for p in parts]

    def times(left, right):
        return lax.dot_general(
            left, right, (((1,), (1,)), ((), ())), preferred_element_type=jnp.float32
        )

    def slot_of(tile, live):
        return jnp.where(live & (tile >= 0), tile - base, slots)

    def home_evaluate(b):
        return evaluate(b, -offset_v[pl.ds(b, 1), :], True)

    def home_reduce(b, buf):
        tiles, _, own = entries(b)
        hit = home_key == own * 8 + species_v[pl.ds(b, 1), :]
        for layer in range(2):
            amp = jnp.broadcast_to(amp_ref[layer, pl.ds(b, 1), :], home_row.shape)
            high = amp.astype(jnp.bfloat16).astype(jnp.float32)
            part = jnp.where(home_rest, amp - high, high)
            left = jnp.where(hit, part, 0.0).astype(jnp.bfloat16)
            sums = times(jnp.concatenate([left, left], axis=1), buf[layer])
            for j in range(NEAR):
                home_acc[layer][slot_of(tiles[j], True)] += sums[8 * j : 8 * j + 8]

    def decode(i):
        code = list_ref[i]
        return lax.shift_right_logical(code, 2), code & 3

    def away_evaluate(i):
        sides = []
        for k in range(2):
            b, r = decode(2 * i + k)
            tiles, count, own = entries(b)
            apart = chosen(rotated(own, count, r), tiles) - chosen(own, tiles)
            shift = (apart * TILE).astype(jnp.float32) - offset_v[pl.ds(b, 1), :]
            sides.append(evaluate(b, shift, False))
        return [jnp.concatenate(both, axis=1) for both in zip(*sides)]

    def away_reduce(i, buf):
        items = []
        for k in range(2):
            b, r = decode(2 * i + k)
            tiles, count, own = entries(b)
            key = rotated(own, count, r) * 4 + species_v[pl.ds(b, 1), :]
            items.append((b, away_key == key, [slot_of(tile, r > 0) for tile in tiles]))
        empty = jnp.zeros(away_key.shape, jnp.bfloat16)
        for layer in range(2):
            left = [
                jnp.where(
                    hit, jnp.broadcast_to(amp_ref[layer, pl.ds(b, 1), :], away_key.shape), 0.0
                ).astype(jnp.bfloat16)
                for b, hit, _ in items
            ]
            stacked = jnp.concatenate(
                [
                    jnp.concatenate([left[0], empty], axis=1),
                    jnp.concatenate([empty, left[1]], axis=1),
                ],
                axis=0,
            )
            sums = times(stacked, buf[layer])
            for k, (_, _, slot) in enumerate(items):
                for j in range(NEAR):
                    at = 16 * k + 8 * (j // 2)
                    part = sums[at : at + 8]
                    part = jnp.where(upper_half, part, 0.0) if j % 2 else jnp.where(upper_half, 0.0, part)
                    away_acc[layer][slot[j]] += part

    def in_batches(batch, first, turns, evaluate_one, reduce_one):
        def step(i, carry):
            for k in range(batch):
                at = first + batch * i + k
                reduce_one(at, evaluate_one(at))
            return carry

        lax.fori_loop(0, turns, step, 0)

    in_batches(HOME_BATCH, 0, blocks // HOME_BATCH, home_evaluate, home_reduce)
    units = lax.shift_right_logical(found + 1, 1)
    full = lax.div(units, AWAY_BATCH)
    in_batches(AWAY_BATCH, 0, full, away_evaluate, away_reduce)
    rest = lax.div(units - AWAY_BATCH * full + TAIL_BATCH - 1, TAIL_BATCH)
    in_batches(TAIL_BATCH, AWAY_BATCH * full, rest, away_evaluate, away_reduce)

    even = (group & 1) == 0
    for slot in range(OWN_TILES):
        at = slot * TILE
        for layer in range(2):
            parts = []
            for third in range(3):
                home = home_acc[layer][third * OWN_TILES + slot]
                away = away_acc[layer][third * OWN_TILES + slot]
                parts.append(
                    home[:SPECIES]
                    + home[SPECIES : 2 * SPECIES]
                    + (away[:SPECIES] + away[4 : 4 + SPECIES])
                )
            where = (slice(SPECIES * layer, SPECIES * (layer + 1)), slice(at, at + TILE))
            outs[0][where] = jnp.where(even, parts[2], parts[0])
            outs[1][where] = parts[1]
            outs[2][where] = jnp.where(even, parts[0], parts[2])


def pair_sums(near, press, temper, lines):
    blocks = near.shape[1]
    row_count = 2 * SPECIES
    vmem = pl.BlockSpec(memory_space=pltpu.VMEM)
    hbm = pl.BlockSpec(memory_space=pltpu.HBM)
    block_shape = (blocks, LBLK)
    f32 = functools.partial(pltpu.VMEM, dtype=jnp.float32)
    sums = jax.ShapeDtypeStruct((row_count, OWN_TILES * TILE), jnp.float32)
    return pl.pallas_call(
        pairs_kernel,
        out_shape=(sums,) * 3,
        in_specs=[hbm] * 9,
        out_specs=[vmem] * 3,
        scratch_shapes=[pltpu.SMEM(near.shape, jnp.int32), f32((1, 2)), f32((1, 2))]
        + [f32(block_shape)] * 5
        + [
            pltpu.VMEM(block_shape, jnp.int32),
            pltpu.SemaphoreType.DMA((9,)),
            f32((2,) + block_shape),
            f32((2,) + block_shape),
            f32((2,) + block_shape),
            f32((TILE, LBLK)),
            pltpu.SMEM((blocks * (NEAR - 1) + 2 * TAIL_BATCH,), jnp.int32),
        ]
        + [f32((3 * OWN_TILES + 1, 8, TILE))] * 4,
        name="pair_sums",
    )(near, press.reshape(1, 2), temper.reshape(1, 2), *[v.reshape(block_shape) for v in lines])


def amounts_kernel(
    points,
    index_ref,
    table_ref,
    noise_ref,
    own_ref,
    other_ref,
    amounts_ref,
    factor_ref,
    scale_ref,
    own_out,
    other_out,
):
    own_out[...] = own_ref[...]
    other_out[...] = other_ref[...]
    scale_ref[...] = (1.0 / points) / noise_ref[...]
    layers, sounds = index_ref.shape
    kinds, entries = table_ref.shape
    entry = lax.broadcasted_iota(jnp.int32, (entries, sounds), 0)
    for layer in range(layers):
        hit = (entry == index_ref[layer : layer + 1, :]).astype(jnp.float32)
        amounts_ref[kinds * layer : kinds * (layer + 1), :] = jnp.dot(
            table_ref[...], hit, precision=HIGH, preferred_element_type=jnp.float32
        )
    amounts = amounts_ref[...]
    own = factor_ref.shape[0]
    first = own * own_place()[1]
    for a in range(own):
        factor_ref[a] = amounts * amounts_ref[pl.ds(first + a, 1), :]


def amount_tables(points, index, table, noise, own, other):
    layers, sounds = index.shape
    columns = layers * SPECIES
    vmem = pl.BlockSpec(memory_space=pltpu.VMEM)
    return pl.pallas_call(
        functools.partial(amounts_kernel, points),
        out_shape=(
            jax.ShapeDtypeStruct((columns, sounds), jnp.float32),
            jax.ShapeDtypeStruct((2 * SPECIES, columns, sounds), jnp.float32),
            jax.ShapeDtypeStruct((1, noise.shape[0]), jnp.float32),
            jax.ShapeDtypeStruct(own.shape, jnp.float32),
            jax.ShapeDtypeStruct(other.shape, jnp.float32),
        ),
        in_specs=[vmem] * 5,
        out_specs=[vmem] * 5,
        compiler_params=pltpu.CompilerParams(vmem_limit_bytes=VMEM_BYTES),
        cost_estimate=pl.CostEstimate(flops=2_000_000, bytes_accessed=100_000, transcendentals=0),
        name="amount_tables",
    )(index, table, noise.reshape(1, -1), own, other)


def gram_kernel(all_ref, amounts_ref, factor_ref, scale_ref, transmit_ref, out_ref):
    lays, own = all_ref.shape[1:3]
    cross = jnp.concatenate([all_ref[0, i] + all_ref[1, i] for i in range(lays)], axis=0)
    depth = lax.dot_general(
        amounts_ref[...],
        cross,
        (((0,), (0,)), ((), ())),
        precision=HIGH,
        preferred_element_type=jnp.float32,
    )
    passed = jnp.exp(-depth)
    transmit_ref[...] = passed
    weight = passed * passed * scale_ref[...]
    lay = own_place()[1]
    mine = all_ref[0, lay] + all_ref[1, lay]
    for a in range(own):
        scaled = weight * mine[a : a + 1, :]
        gram = lax.dot_general(
            cross,
            scaled,
            (((1,), (1,)), ((), ())),
            precision=HIGH,
            preferred_element_type=jnp.float32,
        )
        out_ref[a] = gram * factor_ref[a]


def gram_parts(cross_all, amounts, factor, scale):
    sounds = amounts.shape[1]
    width = scale.shape[1]
    vmem = pl.BlockSpec(memory_space=pltpu.VMEM)
    return pl.pallas_call(
        gram_kernel,
        out_shape=(
            jax.ShapeDtypeStruct((sounds, width), jnp.float32),
            jax.ShapeDtypeStruct(factor.shape, jnp.float32),
        ),
        in_specs=[vmem] * 4,
        out_specs=[vmem] * 2,
        compiler_params=pltpu.CompilerParams(vmem_limit_bytes=VMEM_BYTES),
        name="gram_parts",
    )(cross_all, amounts, factor, scale)


def body(
    line_offset,
    line_strength,
    lower_energy,
    lorentz_width,
    doppler_width,
    line_species,
    cutoff,
    layer_pressure,
    layer_temp,
    column_index,
    column_table,
    noise_var,
):
    groups = lax.axis_size(GROUP)
    lines = (
        line_offset,
        line_strength,
        lower_energy,
        lorentz_width,
        doppler_width,
        line_species,
    )
    first, middle, second = pair_sums(cutoff.T, layer_pressure, layer_temp, lines)
    landed = exchanged(first)
    points = noise_var.shape[0] * groups
    amounts, factor, scale, middle, second = amount_tables(
        points, column_index.T, column_table, noise_var, middle, second
    )
    cross_all = all_layers(middle + landed, second, groups)
    transmit, partial = gram_parts(cross_all, amounts, factor, scale)
    flat = partial.reshape(-1, 128)
    stride = 1
    while stride < groups:
        size = min(8, groups // stride)
        copies = jnp.broadcast_to(flat[None], (size,) + flat.shape)
        flat = summed_over(copies, groups, size, stride)
        stride *= size
    normals = flat.reshape(partial.shape).transpose(2, 0, 1)
    return (transmit, normals)


def solution(mesh):
    in_specs = (
        P(GROUP),
        P(GROUP),
        P(GROUP),
        P(GROUP),
        P(GROUP),
        P(GROUP),
        P(GROUP, None),
        P("lay"),
        P("lay"),
        P(),
        P(),
        P(GROUP),
    )
    out_specs = (P(None, GROUP), P(None, "lay", None))
    return jax.shard_map(body, mesh=mesh, in_specs=in_specs, out_specs=out_specs, check_vma=False)
```

```python
import functools
import math

import jax
import jax.numpy as jnp
from jax import lax
from jax.experimental import pallas as pl
from jax.experimental.pallas import tpu as pltpu
from jax.sharding import PartitionSpec as P

TILE = 256
LBLK = 128
NEAR = 4
SPECIES = 3
OWN_TILES = 4
ROWS = 2 * SPECIES
HOME_BATCH = 32
AWAY_BATCH = 8
TAIL_BATCH = 4
GROUP = ("spec", "line")

HIGH = lax.Precision.HIGHEST
LN_TWO = math.log(2.0)
C_TWO = 1.4388
VMEM_BYTES = 40 * 1024 * 1024


def exchanged(value):
    pairs = [(i, i ^ 1) for i in range(lax.axis_size(GROUP))]
    return lax.ppermute(value, GROUP, pairs)


def all_layers(own, other, groups):
    lays = lax.axis_size("lay")
    members = [
        [lays * (d % groups) + i for d in (odd, odd + 1) for i in range(lays)]
        for odd in range(1, groups, 2)
    ]
    is_odd = (lax.axis_index(GROUP) & 1) == 1
    halves = jnp.stack([jnp.where(is_odd, own, other), jnp.where(is_odd, other, own)])
    copies = jnp.broadcast_to(halves[:, None], (2, lays) + own.shape)
    landed = lax.all_to_all(
        copies.reshape((2 * lays,) + own.shape),
        GROUP + ("lay",),
        0,
        0,
        axis_index_groups=members,
        tiled=True,
    )
    return landed.reshape(copies.shape)


def summed_over(copies, total, size, stride):
    members = [
        [base + stride * k for k in range(size)]
        for base in range(total)
        if (base // stride) % size == 0
    ]
    landed = lax.all_to_all(copies, GROUP, 0, 0, axis_index_groups=members, tiled=True)
    return jnp.sum(landed, axis=0)


def line_tables(press, temper, strength, energy, lwidth, dwidth, rate_ref, mix_ref, amp_ref):
    shape = strength.shape
    for layer in range(2):
        temp = jnp.broadcast_to(temper[:, layer : layer + 1], shape)
        pressure = jnp.broadcast_to(press[:, layer : layer + 1], shape)
        ratio = 296.0 / temp
        lor = lwidth * (pressure * jnp.exp(0.75 * jnp.log(ratio)))
        gau = dwidth * jnp.sqrt(temp / 296.0)
        line = strength * jnp.exp(-C_TWO * energy * (1.0 / temp - 1.0 / 296.0))
        g2 = gau * gau
        g4 = g2 * g2
        l2 = lor * lor
        l4 = l2 * l2
        total = (
            g4 * gau
            + 2.69269 * g4 * lor
            + 2.42843 * g2 * gau * l2
            + 4.47163 * g2 * lor * l2
            + 0.07842 * gau * l4
            + l4 * lor
        )
        width = jnp.exp(0.2 * jnp.log(total))
        inverse = 1.0 / width
        part = lor * inverse
        eta = part * (1.36603 + part * (-0.47719 + part * 0.11116))
        peak = eta * (2.0 / math.pi)
        rate_ref[layer] = -4.0 * inverse * inverse
        mix_ref[layer] = (1.0 - eta) * math.sqrt(4.0 * LN_TWO / math.pi) / peak
        amp_ref[layer] = line * peak * inverse


def own_place():
    return lax.axis_index(GROUP), lax.axis_index("lay")


def pairs_kernel(*refs):
    hbm, outs, scratch = refs[:9], refs[9:12], refs[12:]
    vmem, sems = scratch[:9], scratch[9]
    near, press_v, temper_v, offset_v, strength_v, energy_v, lwidth_v, dwidth_v, species_v = vmem
    rate_ref, mix_ref, amp_ref, point_ref, list_ref = scratch[10:15]
    home_acc, away_acc = scratch[15:17], scratch[17:19]
    copies = [pltpu.make_async_copy(s, d, sems.at[i]) for i, (s, d) in enumerate(zip(hbm, vmem))]
    for copy in copies:
        copy.start()
    for acc in home_acc + away_acc:
        acc[...] = jnp.zeros_like(acc)
    point_ref[...] = lax.broadcasted_iota(jnp.int32, point_ref.shape, 0).astype(jnp.float32)

    slots = home_acc[0].shape[0] - 1
    blocks = near.shape[1]
    group = own_place()[0]
    base = (group - 1) * OWN_TILES
    copies[0].wait()
    for copy in copies[1:]:
        copy.wait()
    line_tables(
        press_v[...],
        temper_v[...],
        strength_v[...],
        energy_v[...],
        lwidth_v[...],
        dwidth_v[...],
        rate_ref,
        mix_ref,
        amp_ref,
    )

    lane = lax.broadcasted_iota(jnp.int32, (1, LBLK), 1)
    lane_three = lax.rem(lane, 3)
    home_row = lax.broadcasted_iota(jnp.int32, (NEAR * 8, LBLK), 0)
    home_part = home_row & 7
    home_rest = home_part >= SPECIES
    home_key = jnp.where(
        home_part < 2 * SPECIES, home_row - jnp.where(home_rest, SPECIES, 0), -1
    )
    away_key = lax.broadcasted_iota(jnp.int32, (NEAR * 4, LBLK), 0)
    upper_half = lax.broadcasted_iota(jnp.int32, (8, TILE), 0) >= 4

    def entries(b):
        tiles = [near[j, b] for j in range(NEAR)]
        count = jnp.int32(1)
        for j in range(1, NEAR):
            count = count + (tiles[j] >= 0).astype(jnp.int32)
        own = jnp.where(count == 3, lane_three, lane & jnp.where(count == 4, 3, count - 1))
        return tiles, count, own

    def rotated(own, count, r):
        entry = own + r
        return jnp.where(entry >= count, entry - count, entry)

    def chosen(entry, tiles):
        tile = jnp.where(entry == 0, tiles[0], tiles[NEAR - 1])
        for j in range(1, NEAR - 1):
            tile = jnp.where(entry == j, tiles[j], tile)
        return tile

    def evaluate(b, shift, split):
        shape = (16, LBLK)
        shift = jnp.broadcast_to(shift, shape)
        rate = [jnp.broadcast_to(rate_ref[layer, pl.ds(b, 1), :], shape) for layer in range(2)]
        mix = [jnp.broadcast_to(mix_ref[layer, pl.ds(b, 1), :], shape) for layer in range(2)]
        parts = [[], []]
        for k in range(0, TILE, 16):
            x = point_ref[k : k + 16, :] + shift
            square = x * x
            for layer in range(2):
                q = square * rate[layer]
                value = 1.0 / (1.0 - q) + mix[layer] * jnp.exp2(q)
                high = value.astype(jnp.bfloat16)
                if split:
                    low = (value - high.astype(jnp.float32)).astype(jnp.bfloat16)
                    high = jnp.concatenate([high, low], axis=1)
                parts[layer].append(high)
        return [jnp.concatenate(p, axis=0) for p in parts]

    def times(left, right):
        return lax.dot_general(
            left, right, (((1,), (1,)), ((), ())), preferred_element_type=jnp.float32
        )

    def slot_of(tile, live):
        return jnp.where(live & (tile >= 0), tile - base, slots)

    def home_evaluate(b):
        return evaluate(b, -offset_v[pl.ds(b, 1), :], True)

    def home_reduce(b, buf):
        tiles, _, own = entries(b)
        hit = home_key == own * 8 + species_v[pl.ds(b, 1), :]
        for layer in range(2):
            amp = jnp.broadcast_to(amp_ref[layer, pl.ds(b, 1), :], home_row.shape)
            high = amp.astype(jnp.bfloat16).astype(jnp.float32)
            part = jnp.where(home_rest, amp - high, high)
            left = jnp.where(hit, part, 0.0).astype(jnp.bfloat16)
            sums = times(jnp.concatenate([left, left], axis=1), buf[layer])
            for j in range(NEAR):
                home_acc[layer][slot_of(tiles[j], True)] += sums[8 * j : 8 * j + 8]

    def decode(i):
        code = list_ref[i]
        return lax.shift_right_logical(code, 2), code & 3

    def away_evaluate(i):
        sides = []
        for k in range(2):
            b, r = decode(2 * i + k)
            tiles, count, own = entries(b)
            apart = chosen(rotated(own, count, r), tiles) - chosen(own, tiles)
            shift = (apart * TILE).astype(jnp.float32) - offset_v[pl.ds(b, 1), :]
            sides.append(evaluate(b, shift, False))
        return [jnp.concatenate(both, axis=1) for both in zip(*sides)]

    def away_reduce(i, buf):
        items = []
        for k in range(2):
            b, r = decode(2 * i + k)
            tiles, count, own = entries(b)
            key = rotated(own, count, r) * 4 + species_v[pl.ds(b, 1), :]
            items.append((b, away_key == key, [slot_of(tile, r > 0) for tile in tiles]))
        empty = jnp.zeros(away_key.shape, jnp.bfloat16)
        for layer in range(2):
            left = [
                jnp.where(
                    hit, jnp.broadcast_to(amp_ref[layer, pl.ds(b, 1), :], away_key.shape), 0.0
                ).astype(jnp.bfloat16)
                for b, hit, _ in items
            ]
            stacked = jnp.concatenate(
                [
                    jnp.concatenate([left[0], empty], axis=1),
                    jnp.concatenate([empty, left[1]], axis=1),
                ],
                axis=0,
            )
            sums = times(stacked, buf[layer])
            for k, (_, _, slot) in enumerate(items):
                for j in range(NEAR):
                    at = 16 * k + 8 * (j // 2)
                    part = sums[at : at + 8]
                    part = jnp.where(upper_half, part, 0.0) if j % 2 else jnp.where(upper_half, 0.0, part)
                    away_acc[layer][slot[j]] += part

    def in_batches(batch, first, turns, evaluate_one, reduce_one):
        def step(i, carry):
            for k in range(batch):
                at = first + batch * i + k
                reduce_one(at, evaluate_one(at))
            return carry

        lax.fori_loop(0, turns, step, 0)

    def home_step(i, found):
        for k in range(HOME_BATCH):
            b = HOME_BATCH * i + k
            home_reduce(b, home_evaluate(b))
            for j in range(1, NEAR):
                list_ref[found] = NEAR * b + j
                found = found + (near[j, b] >= 0).astype(jnp.int32)
        return found

    found = lax.fori_loop(0, blocks // HOME_BATCH, home_step, jnp.int32(0))
    for k in range(2 * TAIL_BATCH):
        list_ref[found + k] = jnp.int32(0)
    units = lax.shift_right_logical(found + 1, 1)
    full = lax.div(units, AWAY_BATCH)
    in_batches(AWAY_BATCH, 0, full, away_evaluate, away_reduce)
    rest = lax.div(units - AWAY_BATCH * full + TAIL_BATCH - 1, TAIL_BATCH)
    in_batches(TAIL_BATCH, AWAY_BATCH * full, rest, away_evaluate, away_reduce)

    even = (group & 1) == 0
    for slot in range(OWN_TILES):
        for layer in range(2):
            parts = []
            for third in range(3):
                home = home_acc[layer][third * OWN_TILES + slot]
                away = away_acc[layer][third * OWN_TILES + slot]
                parts.append(
                    home[:SPECIES]
                    + home[SPECIES : 2 * SPECIES]
                    + (away[:SPECIES] + away[4 : 4 + SPECIES])
                )
            for half in range(TILE // LBLK):
                lanes = slice(half * LBLK, (half + 1) * LBLK)
                piece = [part[:, lanes] for part in parts]
                start = (2 * slot + half) * ROWS + SPECIES * layer
                where = slice(start, start + SPECIES)
                outs[0][where, :] = jnp.where(even, piece[2], piece[0])
                outs[1][where, :] = piece[1]
                outs[2][where, :] = jnp.where(even, piece[0], piece[2])


def pair_sums(near, press, temper, lines):
    blocks = near.shape[1]
    vmem = pl.BlockSpec(memory_space=pltpu.VMEM)
    hbm = pl.BlockSpec(memory_space=pltpu.HBM)
    block_shape = (blocks, LBLK)
    f32 = functools.partial(pltpu.VMEM, dtype=jnp.float32)
    sums = jax.ShapeDtypeStruct((ROWS * OWN_TILES * TILE // LBLK, LBLK), jnp.float32)
    return pl.pallas_call(
        pairs_kernel,
        out_shape=(sums,) * 3,
        in_specs=[hbm] * 9,
        out_specs=[vmem] * 3,
        scratch_shapes=[pltpu.SMEM(near.shape, jnp.int32), f32((1, 2)), f32((1, 2))]
        + [f32(block_shape)] * 5
        + [
            pltpu.VMEM(block_shape, jnp.int32),
            pltpu.SemaphoreType.DMA((9,)),
            f32((2,) + block_shape),
            f32((2,) + block_shape),
            f32((2,) + block_shape),
            f32((TILE, LBLK)),
            pltpu.SMEM((blocks * (NEAR - 1) + 2 * TAIL_BATCH,), jnp.int32),
        ]
        + [f32((3 * OWN_TILES + 1, 8, TILE))] * 4,
        name="pair_sums",
    )(near, press.reshape(1, 2), temper.reshape(1, 2), *[v.reshape(block_shape) for v in lines])


def amounts_kernel(
    points,
    index_ref,
    table_ref,
    noise_ref,
    own_ref,
    other_ref,
    amounts_ref,
    factor_ref,
    scale_ref,
    own_out,
    other_out,
):
    own_out[...] = own_ref[...]
    other_out[...] = other_ref[...]
    scale_ref[...] = (1.0 / points) / noise_ref[...]
    layers, sounds = index_ref.shape
    kinds, entries = table_ref.shape
    entry = lax.broadcasted_iota(jnp.int32, (entries, sounds), 0)
    for layer in range(layers):
        hit = (entry == index_ref[layer : layer + 1, :]).astype(jnp.float32)
        amounts_ref[kinds * layer : kinds * (layer + 1), :] = jnp.dot(
            table_ref[...], hit, precision=HIGH, preferred_element_type=jnp.float32
        )
    amounts = amounts_ref[...]
    own = factor_ref.shape[0]
    first = own * own_place()[1]
    for a in range(own):
        factor_ref[a] = amounts * amounts_ref[pl.ds(first + a, 1), :]


def amount_tables(points, index, table, noise, own, other):
    layers, sounds = index.shape
    columns = layers * SPECIES
    vmem = pl.BlockSpec(memory_space=pltpu.VMEM)
    return pl.pallas_call(
        functools.partial(amounts_kernel, points),
        out_shape=(
            jax.ShapeDtypeStruct((columns, sounds), jnp.float32),
            jax.ShapeDtypeStruct((2 * SPECIES, columns, sounds), jnp.float32),
            jax.ShapeDtypeStruct((1, noise.shape[0]), jnp.float32),
            jax.ShapeDtypeStruct(own.shape, jnp.float32),
            jax.ShapeDtypeStruct(other.shape, jnp.float32),
        ),
        in_specs=[vmem] * 5,
        out_specs=[vmem] * 5,
        compiler_params=pltpu.CompilerParams(vmem_limit_bytes=VMEM_BYTES),
        cost_estimate=pl.CostEstimate(flops=2_000_000, bytes_accessed=100_000, transcendentals=0),
        name="amount_tables",
    )(index, table, noise.reshape(1, -1), own, other)


def gram_kernel(all_ref, amounts_ref, factor_ref, scale_ref, transmit_ref, out_ref):
    lays = all_ref.shape[1]
    cuts = range(0, all_ref.shape[2], ROWS)
    parts = [all_ref[0, i] + all_ref[1, i] for i in range(lays)]
    cross = jnp.concatenate(
        [jnp.concatenate([p[c : c + ROWS] for p in parts], axis=0) for c in cuts], axis=1
    )
    depth = lax.dot_general(
        amounts_ref[...],
        cross,
        (((0,), (0,)), ((), ())),
        precision=HIGH,
        preferred_element_type=jnp.float32,
    )
    passed = jnp.exp(-depth)
    transmit_ref[...] = passed
    weight = passed * passed * scale_ref[...]
    lay = own_place()[1]
    mine = all_ref[0, lay] + all_ref[1, lay]
    mine = jnp.concatenate([mine[c : c + ROWS] for c in cuts], axis=1)
    for a in range(ROWS):
        scaled = weight * mine[a : a + 1, :]
        gram = lax.dot_general(
            cross,
            scaled,
            (((1,), (1,)), ((), ())),
            precision=HIGH,
            preferred_element_type=jnp.float32,
        )
        out_ref[a] = gram * factor_ref[a]


def gram_parts(cross_all, amounts, factor, scale):
    sounds = amounts.shape[1]
    width = scale.shape[1]
    vmem = pl.BlockSpec(memory_space=pltpu.VMEM)
    return pl.pallas_call(
        gram_kernel,
        out_shape=(
            jax.ShapeDtypeStruct((sounds, width), jnp.float32),
            jax.ShapeDtypeStruct(factor.shape, jnp.float32),
        ),
        in_specs=[vmem] * 4,
        out_specs=[vmem] * 2,
        compiler_params=pltpu.CompilerParams(vmem_limit_bytes=VMEM_BYTES),
        name="gram_parts",
    )(cross_all, amounts, factor, scale)


def body(
    line_offset,
    line_strength,
    lower_energy,
    lorentz_width,
    doppler_width,
    line_species,
    cutoff,
    layer_pressure,
    layer_temp,
    column_index,
    column_table,
    noise_var,
):
    groups = lax.axis_size(GROUP)
    lines = (
        line_offset,
        line_strength,
        lower_energy,
        lorentz_width,
        doppler_width,
        line_species,
    )
    first, middle, second = pair_sums(cutoff.T, layer_pressure, layer_temp, lines)
    landed = exchanged(first)
    points = noise_var.shape[0] * groups
    amounts, factor, scale, middle, second = amount_tables(
        points, column_index.T, column_table, noise_var, middle, second
    )
    cross_all = all_layers(middle + landed, second, groups)
    transmit, partial = gram_parts(cross_all, amounts, factor, scale)
    flat = partial.reshape(-1, 128)
    stride = 1
    while stride < groups:
        size = min(8, groups // stride)
        copies = jnp.broadcast_to(flat[None], (size,) + flat.shape)
        flat = summed_over(copies, groups, size, stride)
        stride *= size
    normals = flat.reshape(partial.shape).transpose(2, 0, 1)
    return (transmit, normals)


def solution(mesh):
    in_specs = (
        P(GROUP),
        P(GROUP),
        P(GROUP),
        P(GROUP),
        P(GROUP),
        P(GROUP),
        P(GROUP, None),
        P("lay"),
        P("lay"),
        P(),
        P(),
        P(GROUP),
    )
    out_specs = (P(None, GROUP), P(None, "lay", None))
    return jax.shard_map(body, mesh=mesh, in_specs=in_specs, out_specs=out_specs, check_vma=False)
```

```python
import functools
import math

import jax
import jax.numpy as jnp
from jax import lax
from jax.experimental import pallas as pl
from jax.experimental.pallas import tpu as pltpu
from jax.sharding import PartitionSpec as P

TILE = 256
LBLK = 128
NEAR = 4
SPECIES = 3
OWN_TILES = 4
ROWS = 2 * SPECIES
HOME_BATCH = 32
AWAY_BATCHES = (16, 8, 4)
GROUP = ("spec", "line")

HIGH = lax.Precision.HIGHEST
LN_TWO = math.log(2.0)
C_TWO = 1.4388
VMEM_BYTES = 40 * 1024 * 1024


def exchanged(value):
    pairs = [(i, i ^ 1) for i in range(lax.axis_size(GROUP))]
    return lax.ppermute(value, GROUP, pairs)


def all_layers(own, other, groups):
    lays = lax.axis_size("lay")
    members = [
        [lays * (d % groups) + i for d in (odd, odd + 1) for i in range(lays)]
        for odd in range(1, groups, 2)
    ]
    is_odd = (lax.axis_index(GROUP) & 1) == 1
    halves = jnp.stack([jnp.where(is_odd, own, other), jnp.where(is_odd, other, own)])
    copies = jnp.broadcast_to(halves[:, None], (2, lays) + own.shape)
    landed = lax.all_to_all(
        copies.reshape((2 * lays,) + own.shape),
        GROUP + ("lay",),
        0,
        0,
        axis_index_groups=members,
        tiled=True,
    )
    return landed.reshape(copies.shape)


def summed_over(copies, total, size, stride):
    members = [
        [base + stride * k for k in range(size)]
        for base in range(total)
        if (base // stride) % size == 0
    ]
    landed = lax.all_to_all(copies, GROUP, 0, 0, axis_index_groups=members, tiled=True)
    return jnp.sum(landed, axis=0)


def line_tables(press, temper, strength, energy, lwidth, dwidth, rate_ref, mix_ref, amp_ref):
    shape = strength.shape
    for layer in range(2):
        temp = jnp.broadcast_to(temper[:, layer : layer + 1], shape)
        pressure = jnp.broadcast_to(press[:, layer : layer + 1], shape)
        ratio = 296.0 / temp
        lor = lwidth * (pressure * jnp.exp(0.75 * jnp.log(ratio)))
        gau = dwidth * jnp.sqrt(temp / 296.0)
        line = strength * jnp.exp(-C_TWO * energy * (1.0 / temp - 1.0 / 296.0))
        g2 = gau * gau
        g4 = g2 * g2
        l2 = lor * lor
        l4 = l2 * l2
        total = (
            g4 * gau
            + 2.69269 * g4 * lor
            + 2.42843 * g2 * gau * l2
            + 4.47163 * g2 * lor * l2
            + 0.07842 * gau * l4
            + l4 * lor
        )
        width = jnp.exp(0.2 * jnp.log(total))
        inverse = 1.0 / width
        part = lor * inverse
        eta = part * (1.36603 + part * (-0.47719 + part * 0.11116))
        peak = eta * (2.0 / math.pi)
        rate_ref[layer] = -4.0 * inverse * inverse
        mix_ref[layer] = (1.0 - eta) * math.sqrt(4.0 * LN_TWO / math.pi) / peak
        amp_ref[layer] = line * peak * inverse


def own_place():
    return lax.axis_index(GROUP), lax.axis_index("lay")


def pairs_kernel(*refs):
    hbm, outs, scratch = refs[:9], refs[9:12], refs[12:]
    vmem, sems = scratch[:9], scratch[9]
    near, press_v, temper_v, offset_v, strength_v, energy_v, lwidth_v, dwidth_v, species_v = vmem
    rate_ref, mix_ref, amp_ref, point_ref, list_ref = scratch[10:15]
    home_acc, away_acc = scratch[15:17], scratch[17:19]
    copies = [pltpu.make_async_copy(s, d, sems.at[i]) for i, (s, d) in enumerate(zip(hbm, vmem))]
    for copy in copies:
        copy.start()
    for acc in home_acc + away_acc:
        acc[...] = jnp.zeros_like(acc)
    point_ref[...] = lax.broadcasted_iota(jnp.int32, point_ref.shape, 0).astype(jnp.float32)

    slots = home_acc[0].shape[0] - 1
    blocks = near.shape[1]
    group = own_place()[0]
    base = (group - 1) * OWN_TILES
    copies[0].wait()
    for copy in copies[1:]:
        copy.wait()
    line_tables(
        press_v[...],
        temper_v[...],
        strength_v[...],
        energy_v[...],
        lwidth_v[...],
        dwidth_v[...],
        rate_ref,
        mix_ref,
        amp_ref,
    )

    lane = lax.broadcasted_iota(jnp.int32, (1, LBLK), 1)
    lane_three = lax.rem(lane, 3)
    home_row = lax.broadcasted_iota(jnp.int32, (NEAR * 8, LBLK), 0)
    home_part = home_row & 7
    home_rest = home_part >= SPECIES
    home_key = jnp.where(
        home_part < 2 * SPECIES, home_row - jnp.where(home_rest, SPECIES, 0), -1
    )
    away_key = lax.broadcasted_iota(jnp.int32, (NEAR * 4, LBLK), 0)
    upper_half = lax.broadcasted_iota(jnp.int32, (8, TILE), 0) >= 4

    def entries(b):
        tiles = [near[j, b] for j in range(NEAR)]
        count = jnp.int32(1)
        for j in range(1, NEAR):
            count = count + (tiles[j] >= 0).astype(jnp.int32)
        own = jnp.where(count == 3, lane_three, lane & jnp.where(count == 4, 3, count - 1))
        return tiles, count, own

    def rotated(own, count, r):
        entry = own + r
        return jnp.where(entry >= count, entry - count, entry)

    def chosen(entry, tiles):
        tile = jnp.where(entry == 0, tiles[0], tiles[NEAR - 1])
        for j in range(1, NEAR - 1):
            tile = jnp.where(entry == j, tiles[j], tile)
        return tile

    def evaluate(b, shift, split):
        shape = (32, LBLK)
        shift = jnp.broadcast_to(shift, shape)
        rate = [jnp.broadcast_to(rate_ref[layer, pl.ds(b, 1), :], shape) for layer in range(2)]
        mix = [jnp.broadcast_to(mix_ref[layer, pl.ds(b, 1), :], shape) for layer in range(2)]
        parts = [[], []]
        for k in range(0, TILE, 32):
            x = point_ref[k : k + 32, :] + shift
            square = x * x
            for layer in range(2):
                q = square * rate[layer]
                value = 1.0 / (1.0 - q) + mix[layer] * jnp.exp2(q)
                high = value.astype(jnp.bfloat16)
                if split:
                    low = (value - high.astype(jnp.float32)).astype(jnp.bfloat16)
                    high = jnp.concatenate([high, low], axis=1)
                parts[layer].append(high)
        return [jnp.concatenate(p, axis=0) for p in parts]

    def times(left, right):
        return lax.dot_general(
            left, right, (((1,), (1,)), ((), ())), preferred_element_type=jnp.float32
        )

    def slot_of(tile, live):
        return jnp.where(live & (tile >= 0), tile - base, slots)

    def home_evaluate(b):
        return evaluate(b, -offset_v[pl.ds(b, 1), :], True)

    def home_reduce(b, buf):
        tiles, _, own = entries(b)
        hit = home_key == own * 8 + species_v[pl.ds(b, 1), :]
        for layer in range(2):
            amp = jnp.broadcast_to(amp_ref[layer, pl.ds(b, 1), :], home_row.shape)
            high = amp.astype(jnp.bfloat16).astype(jnp.float32)
            part = jnp.where(home_rest, amp - high, high)
            left = jnp.where(hit, part, 0.0).astype(jnp.bfloat16)
            sums = times(jnp.concatenate([left, left], axis=1), buf[layer])
            for j in range(NEAR):
                home_acc[layer][slot_of(tiles[j], True)] += sums[8 * j : 8 * j + 8]

    def decode(i):
        code = list_ref[i]
        return lax.shift_right_logical(code, 2), code & 3

    def away_evaluate(i):
        sides = []
        for k in range(2):
            b, r = decode(2 * i + k)
            tiles, count, own = entries(b)
            apart = chosen(rotated(own, count, r), tiles) - chosen(own, tiles)
            shift = (apart * TILE).astype(jnp.float32) - offset_v[pl.ds(b, 1), :]
            sides.append(evaluate(b, shift, False))
        return [jnp.concatenate(both, axis=1) for both in zip(*sides)]

    def away_reduce(i, buf):
        items = []
        for k in range(2):
            b, r = decode(2 * i + k)
            tiles, count, own = entries(b)
            key = rotated(own, count, r) * 4 + species_v[pl.ds(b, 1), :]
            items.append((b, away_key == key, [slot_of(tile, r > 0) for tile in tiles]))
        empty = jnp.zeros(away_key.shape, jnp.bfloat16)
        for layer in range(2):
            left = [
                jnp.where(
                    hit, jnp.broadcast_to(amp_ref[layer, pl.ds(b, 1), :], away_key.shape), 0.0
                ).astype(jnp.bfloat16)
                for b, hit, _ in items
            ]
            stacked = jnp.concatenate(
                [
                    jnp.concatenate([left[0], empty], axis=1),
                    jnp.concatenate([empty, left[1]], axis=1),
                ],
                axis=0,
            )
            sums = times(stacked, buf[layer])
            for k, (_, _, slot) in enumerate(items):
                for j in range(NEAR):
                    at = 16 * k + 8 * (j // 2)
                    part = sums[at : at + 8]
                    part = jnp.where(upper_half, part, 0.0) if j % 2 else jnp.where(upper_half, 0.0, part)
                    away_acc[layer][slot[j]] += part

    def in_batches(batch, first, turns, evaluate_one, reduce_one):
        def step(i, carry):
            for k in range(batch):
                at = first + batch * i + k
                reduce_one(at, evaluate_one(at))
            return carry

        lax.fori_loop(0, turns, step, 0)

    def home_step(i, found):
        for k in range(HOME_BATCH):
            b = HOME_BATCH * i + k
            home_reduce(b, home_evaluate(b))
            for j in range(1, NEAR):
                list_ref[found] = NEAR * b + j
                found = found + (near[j, b] >= 0).astype(jnp.int32)
        return found

    found = lax.fori_loop(0, blocks // HOME_BATCH, home_step, jnp.int32(0))
    for k in range(2 * AWAY_BATCHES[-1]):
        list_ref[found + k] = jnp.int32(0)
    units = lax.shift_right_logical(found + 1, 1)
    first = jnp.int32(0)
    for batch in AWAY_BATCHES:
        spare = batch - 1 if batch == AWAY_BATCHES[-1] else 0
        turns = lax.div(units - first + spare, batch)
        in_batches(batch, first, turns, away_evaluate, away_reduce)
        first = first + batch * turns

    even = (group & 1) == 0
    for slot in range(OWN_TILES):
        for layer in range(2):
            parts = []
            for third in range(3):
                home = home_acc[layer][third * OWN_TILES + slot]
                away = away_acc[layer][third * OWN_TILES + slot]
                parts.append(
                    home[:SPECIES]
                    + home[SPECIES : 2 * SPECIES]
                    + (away[:SPECIES] + away[4 : 4 + SPECIES])
                )
            for half in range(TILE // LBLK):
                lanes = slice(half * LBLK, (half + 1) * LBLK)
                piece = [part[:, lanes] for part in parts]
                start = (2 * slot + half) * ROWS + SPECIES * layer
                where = slice(start, start + SPECIES)
                outs[0][where, :] = jnp.where(even, piece[2], piece[0])
                outs[1][where, :] = piece[1]
                outs[2][where, :] = jnp.where(even, piece[0], piece[2])


def pair_sums(near, press, temper, lines):
    blocks = near.shape[1]
    vmem = pl.BlockSpec(memory_space=pltpu.VMEM)
    hbm = pl.BlockSpec(memory_space=pltpu.HBM)
    block_shape = (blocks, LBLK)
    f32 = functools.partial(pltpu.VMEM, dtype=jnp.float32)
    sums = jax.ShapeDtypeStruct((ROWS * OWN_TILES * TILE // LBLK, LBLK), jnp.float32)
    return pl.pallas_call(
        pairs_kernel,
        out_shape=(sums,) * 3,
        in_specs=[hbm] * 9,
        out_specs=[vmem] * 3,
        scratch_shapes=[pltpu.SMEM(near.shape, jnp.int32), f32((1, 2)), f32((1, 2))]
        + [f32(block_shape)] * 5
        + [
            pltpu.VMEM(block_shape, jnp.int32),
            pltpu.SemaphoreType.DMA((9,)),
            f32((2,) + block_shape),
            f32((2,) + block_shape),
            f32((2,) + block_shape),
            f32((TILE, LBLK)),
            pltpu.SMEM((blocks * (NEAR - 1) + 2 * AWAY_BATCHES[-1],), jnp.int32),
        ]
        + [f32((3 * OWN_TILES + 1, 8, TILE))] * 4,
        name="pair_sums",
    )(near, press.reshape(1, 2), temper.reshape(1, 2), *[v.reshape(block_shape) for v in lines])


def amounts_kernel(
    points,
    index_ref,
    table_ref,
    noise_ref,
    own_ref,
    other_ref,
    amounts_ref,
    factor_ref,
    scale_ref,
    own_out,
    other_out,
):
    own_out[...] = own_ref[...]
    other_out[...] = other_ref[...]
    scale_ref[...] = (1.0 / points) / noise_ref[...]
    layers, sounds = index_ref.shape
    kinds, entries = table_ref.shape
    entry = lax.broadcasted_iota(jnp.int32, (entries, sounds), 0)
    for layer in range(layers):
        hit = (entry == index_ref[layer : layer + 1, :]).astype(jnp.float32)
        amounts_ref[kinds * layer : kinds * (layer + 1), :] = jnp.dot(
            table_ref[...], hit, precision=HIGH, preferred_element_type=jnp.float32
        )
    amounts = amounts_ref[...]
    own = factor_ref.shape[0]
    first = own * own_place()[1]
    for a in range(own):
        factor_ref[a] = amounts * amounts_ref[pl.ds(first + a, 1), :]


def amount_tables(points, index, table, noise, own, other):
    layers, sounds = index.shape
    columns = layers * SPECIES
    vmem = pl.BlockSpec(memory_space=pltpu.VMEM)
    return pl.pallas_call(
        functools.partial(amounts_kernel, points),
        out_shape=(
            jax.ShapeDtypeStruct((columns, sounds), jnp.float32),
            jax.ShapeDtypeStruct((2 * SPECIES, columns, sounds), jnp.float32),
            jax.ShapeDtypeStruct((1, noise.shape[0]), jnp.float32),
            jax.ShapeDtypeStruct(own.shape, jnp.float32),
            jax.ShapeDtypeStruct(other.shape, jnp.float32),
        ),
        in_specs=[vmem] * 5,
        out_specs=[vmem] * 5,
        compiler_params=pltpu.CompilerParams(vmem_limit_bytes=VMEM_BYTES),
        cost_estimate=pl.CostEstimate(flops=2_000_000, bytes_accessed=100_000, transcendentals=0),
        name="amount_tables",
    )(index, table, noise.reshape(1, -1), own, other)


def gram_kernel(all_ref, amounts_ref, factor_ref, scale_ref, transmit_ref, out_ref):
    lays = all_ref.shape[1]
    cuts = range(0, all_ref.shape[2], ROWS)
    parts = [all_ref[0, i] + all_ref[1, i] for i in range(lays)]
    cross = jnp.concatenate(
        [jnp.concatenate([p[c : c + ROWS] for p in parts], axis=0) for c in cuts], axis=1
    )
    depth = lax.dot_general(
        amounts_ref[...],
        cross,
        (((0,), (0,)), ((), ())),
        precision=HIGH,
        preferred_element_type=jnp.float32,
    )
    passed = jnp.exp(-depth)
    transmit_ref[...] = passed
    weight = passed * passed * scale_ref[...]
    lay = own_place()[1]
    mine = all_ref[0, lay] + all_ref[1, lay]
    mine = jnp.concatenate([mine[c : c + ROWS] for c in cuts], axis=1)
    for a in range(ROWS):
        scaled = weight * mine[a : a + 1, :]
        gram = lax.dot_general(
            cross,
            scaled,
            (((1,), (1,)), ((), ())),
            precision=HIGH,
            preferred_element_type=jnp.float32,
        )
        out_ref[a] = gram * factor_ref[a]


def gram_parts(cross_all, amounts, factor, scale):
    sounds = amounts.shape[1]
    width = scale.shape[1]
    vmem = pl.BlockSpec(memory_space=pltpu.VMEM)
    return pl.pallas_call(
        gram_kernel,
        out_shape=(
            jax.ShapeDtypeStruct((sounds, width), jnp.float32),
            jax.ShapeDtypeStruct(factor.shape, jnp.float32),
        ),
        in_specs=[vmem] * 4,
        out_specs=[vmem] * 2,
        compiler_params=pltpu.CompilerParams(vmem_limit_bytes=VMEM_BYTES),
        name="gram_parts",
    )(cross_all, amounts, factor, scale)


def body(
    line_offset,
    line_strength,
    lower_energy,
    lorentz_width,
    doppler_width,
    line_species,
    cutoff,
    layer_pressure,
    layer_temp,
    column_index,
    column_table,
    noise_var,
):
    groups = lax.axis_size(GROUP)
    lines = (
        line_offset,
        line_strength,
        lower_energy,
        lorentz_width,
        doppler_width,
        line_species,
    )
    first, middle, second = pair_sums(cutoff.T, layer_pressure, layer_temp, lines)
    landed = exchanged(first)
    points = noise_var.shape[0] * groups
    amounts, factor, scale, middle, second = amount_tables(
        points, column_index.T, column_table, noise_var, middle, second
    )
    cross_all = all_layers(middle + landed, second, groups)
    transmit, partial = gram_parts(cross_all, amounts, factor, scale)
    flat = partial.reshape(-1, 128)
    stride = 1
    while stride < groups:
        size = min(8, groups // stride)
        copies = jnp.broadcast_to(flat[None], (size,) + flat.shape)
        flat = summed_over(copies, groups, size, stride)
        stride *= size
    normals = flat.reshape(partial.shape).transpose(2, 0, 1)
    return (transmit, normals)


def solution(mesh):
    in_specs = (
        P(GROUP),
        P(GROUP),
        P(GROUP),
        P(GROUP),
        P(GROUP),
        P(GROUP),
        P(GROUP, None),
        P("lay"),
        P("lay"),
        P(),
        P(),
        P(GROUP),
    )
    out_specs = (P(None, GROUP), P(None, "lay", None))
    return jax.shard_map(body, mesh=mesh, in_specs=in_specs, out_specs=out_specs, check_vma=False)
```
